32 devices in a mesh: tp: 2 (over y), dp: 4 (over z), hg: 4 (over x, core).
Axes of the slice: x: 2, y: 2, z: 4, core: 2. Of those that a mesh axis runs over, the one named last changes fastest.
Arguments:
- hidden_in: bfloat16 [4, 4, 256, 4096], P('dp', 'hg', 'tp'), may hold values from -45 to 45
- norm_gain: float32 [4096], replicated, may hold values from 0.1 to 1.9
- qkv_weight: bfloat16 [4096, 3, 32, 128], P(('dp', 'hg'), None, 'tp'), may hold values from -0.09375 to 0.09375
- out_weight: bfloat16 [32, 128, 4096], P('tp', None, ('dp', 'hg')), may hold values from -0.5 to 0.5
- cache_kv: bfloat16 [4, 32, 1024, 256], P('dp', 'tp'), may hold values from -200 to 200
- cached_lengths: int32 [4], replicated, may hold values from 128 to 1024, as said below
- owner_table: int32 [4, 16], replicated, may hold values from 0 to 3, as said below
Outputs:
- hidden_out: bfloat16 [4, 4, 256, 4096], P('dp', 'hg', 'tp')
- decode_kv: bfloat16 [4, 32, 4, 4, 128, 256], P('dp', ('tp', 'hg'))
The draws below stay inside these ranges and needn't reach their ends.
Inputs may be any that keep to these rules, and one draw needn't show every extreme that they name: `cached_lengths`: multiples of 128; one request has exactly 1024. `owner_table`: a request has at most 4 valid blocks with one owner; one owner holds exactly 4 valid blocks of every request.
All inputs are finite; a program needn't handle non-finite values.
Results may differ from the reference program's by a relative error of at most 0.015.
Values may be sent and summed in bfloat16 or wider, within the bound.
No kernel may reach another device: no remote copies, remote signals or barrier semaphores. Data moves between devices by JAX's collectives and lax.ppermute only.
A program may use at most 128 MiB of HBM per device.

```python
import math
import jax
import jax.numpy as jnp
from jax import lax

D = 4096
HEADS = 32
HD = 128
ROT = 32
STRETCH = 1024
PMAX = 1024
BLOCK = 128
REQS = 4
RUN = 256
NBLK = 16
CAP = 4
N_DP = 4
N_HG = 4


def draw_hidden_in(key, part):
    key_base, key_rows, key_cols = jax.random.split(key, 3)
    full_shape = (REQS, N_HG, RUN, D)
    row_scale = jnp.exp(jax.random.uniform(key_rows, (REQS, N_HG, RUN, 1), jnp.float32, -1.2, 1.2))
    col_scale = jnp.exp(jax.random.uniform(key_cols, (1, 1, 1, D), jnp.float32, -1.2, 1.2))
    base_draw = jnp.clip(jax.random.normal(key_base, full_shape, jnp.float32), -4.0, 4.0)
    return (base_draw * row_scale * col_scale).astype(jnp.bfloat16)


def draw_cache_kv(key, part):
    full_shape = (REQS, HEADS, PMAX, 2 * HD)
    key_base = jax.random.fold_in(key, 0)
    base_draw = jnp.clip(jax.random.normal(key_base, full_shape, jnp.float32), -6.0, 6.0)
    return base_draw.astype(jnp.bfloat16)


def lengths_and_owners(key):
    base_key = jax.random.fold_in(key, 11)
    key_exp, key_add, key_long, key_hot, key_rest = jax.random.split(base_key, 5)
    most_units = PMAX // BLOCK
    top_exp = most_units.bit_length() - 1
    powers = jnp.left_shift(jnp.ones((REQS,), jnp.int32), jax.random.randint(key_exp, (REQS,), 0, top_exp + 1))
    unit_count = jnp.minimum(powers + jax.random.randint(key_add, (REQS,), 0, powers), most_units)
    longest = jax.random.randint(key_long, (), 0, REQS)
    unit_count = jnp.where(jnp.arange(REQS, dtype=jnp.int32) == longest, most_units, unit_count).astype(jnp.int32)
    hot_owner = jax.random.randint(key_hot, (), 0, N_DP).astype(jnp.int32)

    def assign(request_key, used_blocks):
        key_order, key_perm = jax.random.split(request_key)
        block_ids = jnp.arange(NBLK, dtype=jnp.int32)
        shuffle = jax.random.permutation(key_order, NBLK).astype(jnp.int32)
        priority = jnp.where(block_ids < used_blocks, 0, NBLK) + shuffle
        ordering = jnp.argsort(priority, stable=True)
        position_rank = jnp.argsort(ordering, stable=True).astype(jnp.int32)
        owner_perm = jax.random.permutation(key_perm, N_DP).astype(jnp.int32)
        owner_perm = jnp.where(owner_perm == hot_owner, owner_perm[0], owner_perm)
        owner_perm = owner_perm.at[0].set(hot_owner)
        return owner_perm[position_rank // CAP]
    request_keys = jax.random.split(key_rest, REQS)
    owner_rows = jax.vmap(assign)(request_keys, unit_count + STRETCH // BLOCK)
    return ((unit_count * BLOCK).astype(jnp.int32), owner_rows.astype(jnp.int32))


def draw_cached_lengths(key, part):
    return lengths_and_owners(key)[0]


def draw_owner_table(key, part):
    return lengths_and_owners(key)[1]


def block_scale(stream_key, dims, cuts, low, high):
    def one(dim, blocks):
        draws = jax.random.uniform(jax.random.fold_in(jax.random.fold_in(stream_key, 6), dim), (blocks,), jnp.float32, low / len(cuts), high / len(cuts))
        return jnp.repeat(jnp.exp(draws), dims[dim] // blocks).reshape((-1,) + (1,) * (len(dims) - dim - 1))

    factor_of = one(*cuts[0])
    for cut in cuts[1:]:
        factor_of = factor_of * one(*cut)
    return factor_of


def normal_values(stream_key, shape, scale, bound, pieces=(), held_as=jnp.bfloat16):
    gain = block_scale(stream_key, shape, pieces, -0.22, 0.18) if pieces else 1.0
    drawn = jax.random.normal(stream_key, shape, jnp.float32) * scale * gain
    return jnp.minimum(jnp.maximum(drawn, -bound), bound).astype(held_as)


def setup_inputs(seed: int = 0) -> dict:
    keys = jax.random.split(jax.random.key(seed), 8)
    return {
        "hidden_in": draw_hidden_in(jax.random.fold_in(keys[7], 71), 0),
        "norm_gain": jnp.clip(1.0 + 0.18 * jax.random.normal(keys[1], (D,), jnp.float32), 0.1, 1.9),
        "qkv_weight": normal_values(keys[2], (D, 3, HEADS, HD), D ** -0.5, 0.09375, ((0, 16), (2, 2))),
        "out_weight": normal_values(keys[3], (HEADS, HD, D), HD ** -0.5, 0.5, ((0, 2), (2, 16))),
        "cache_kv": draw_cache_kv(jax.random.fold_in(keys[7], 71), 0),
        "cached_lengths": draw_cached_lengths(jax.random.fold_in(keys[7], 71), 0),
        "owner_table": draw_owner_table(jax.random.fold_in(keys[7], 71), 0),
    }


epsilon = 1e-05

def layer_norm(row_data, gain_row):
    row_data = row_data.astype(jnp.float32)
    centered = row_data - lax.optimization_barrier(jnp.mean(row_data, axis=-1, keepdims=True))
    spread = lax.optimization_barrier(jnp.mean(centered * centered, axis=-1, keepdims=True))
    return (centered * lax.rsqrt(spread + epsilon) * gain_row.astype(jnp.float32)).astype(jnp.bfloat16)

def rotate(vectors, positions, rot_dims):
    half_dims = rot_dims // 2
    frequency = 10000.0 ** (-2.0 * jnp.arange(half_dims, dtype=jnp.float32) / rot_dims)
    angles = positions.astype(jnp.float32)[:, None, None] * frequency[None, None, :]
    cosine = jnp.cos(angles)
    sine_part = jnp.sin(angles)
    first_half = vectors[..., :half_dims]
    second = vectors[..., half_dims:rot_dims]
    return jnp.concatenate([first_half * cosine - second * sine_part, second * cosine + first_half * sine_part, vectors[..., rot_dims:]], axis=-1)

def attend(queries, key_rows, value_rows, limit_base):
    scores = jnp.dot(queries, key_rows.T, preferred_element_type=jnp.float32) / math.sqrt(queries.shape[-1])
    row_limit = limit_base + jnp.arange(queries.shape[0], dtype=jnp.int32)
    allowed = jnp.arange(key_rows.shape[0], dtype=jnp.int32)[None, :] <= row_limit[:, None]
    scores = jnp.where(allowed, scores, -jnp.inf)
    row_max = lax.optimization_barrier(jnp.max(scores, axis=1, keepdims=True))
    weights = jnp.exp(scores - row_max)
    row_total = lax.optimization_barrier(jnp.sum(weights, axis=1, keepdims=True))
    attended = jnp.dot(weights.astype(jnp.bfloat16), value_rows, preferred_element_type=jnp.float32) / row_total
    return attended.astype(jnp.bfloat16)

def selector(owner_row, valid_end, low_block, high_block, owner_count, slot_cap):
    block_ids = jnp.arange(owner_row.shape[0], dtype=jnp.int32)
    is_valid = block_ids < valid_end
    same_owner = (owner_row[:, None] == owner_row[None, :]) & is_valid[None, :] & (block_ids[None, :] < block_ids[:, None])
    slot_rank = lax.optimization_barrier(jnp.sum(same_owner.astype(jnp.int32), axis=1))
    chosen = is_valid & (block_ids >= low_block) & (block_ids < high_block)
    slot_ids = jnp.arange(owner_count * slot_cap, dtype=jnp.int32)
    picked = chosen[None, :] & (owner_row[None, :] == (slot_ids // slot_cap)[:, None]) & (slot_rank[None, :] == (slot_ids % slot_cap)[:, None])
    return picked.astype(jnp.bfloat16)

def reference(hidden_in, norm_gain, qkv_weight, out_weight, cache_kv, cached_lengths, owner_table):
    head_width = HEADS * HD
    qkv_flat = qkv_weight.reshape(D, 3 * head_width)
    out_flat = out_weight.reshape(head_width, D)
    zero_index = jnp.zeros((), jnp.int32)
    outputs = []
    handed = []
    for request in range(REQS):
        length = cached_lengths[request]
        row_block = hidden_in[request].reshape(STRETCH, D)
        normed = layer_norm(row_block, norm_gain)
        projected = jnp.dot(normed, qkv_flat, preferred_element_type=jnp.float32)
        positions = length + jnp.arange(STRETCH, dtype=jnp.int32)
        queries = rotate(projected[:, :head_width].reshape(STRETCH, HEADS, HD), positions, ROT).astype(jnp.bfloat16)
        new_keys = rotate(projected[:, head_width:2 * head_width].reshape(STRETCH, HEADS, HD), positions, ROT).astype(jnp.bfloat16)
        new_values = projected[:, 2 * head_width:].reshape(STRETCH, HEADS, HD).astype(jnp.bfloat16)
        stretch_kv = jnp.concatenate([new_keys, new_values], axis=2).transpose(1, 0, 2)
        extended = jnp.concatenate([cache_kv[request], jnp.zeros((HEADS, STRETCH, 2 * HD), jnp.bfloat16)], axis=1)

        def one_head(operands):
            head_queries, head_extended, head_stretch = operands
            sequence = lax.dynamic_update_slice(head_extended, head_stretch, (length.astype(jnp.int32), zero_index))
            return (attend(head_queries, sequence[:, :HD], sequence[:, HD:], length), sequence)
        attended, sequence = lax.map(one_head, (queries.transpose(1, 0, 2), extended, stretch_kv))
        attn_sum = jnp.dot(attended.transpose(1, 0, 2).reshape(STRETCH, head_width), out_flat, preferred_element_type=jnp.float32)
        outputs.append((row_block.astype(jnp.float32) + attn_sum).astype(jnp.bfloat16).reshape(N_HG, RUN, D))
        valid_end = (length + STRETCH) // BLOCK
        picked = selector(owner_table[request], valid_end, 0, NBLK, N_DP, CAP)
        blocks = sequence.reshape(HEADS, NBLK, BLOCK * 2 * HD)
        placed = jnp.einsum('sb,hbx->shx', picked.astype(jnp.float32), blocks.astype(jnp.float32))
        handed.append(placed.astype(jnp.bfloat16).reshape(N_DP, CAP, HEADS, BLOCK, 2 * HD).transpose(0, 2, 1, 3, 4))
    return (jnp.stack(outputs), jnp.stack(handed, axis=2))
```

```python
import math

import jax
import jax.numpy as jnp
from jax import lax
from jax.experimental import pallas as pl
from jax.experimental.pallas import tpu as pltpu
from jax.sharding import PartitionSpec as P

ROT = 32
BLOCK = 128
EPSILON = 1e-05
VMEM_LIMIT = 48 * 1024 * 1024

SMEM = pltpu.SMEM
BF16 = jnp.bfloat16
F32 = jnp.float32


def params():
    return pltpu.CompilerParams(vmem_limit_bytes=VMEM_LIMIT)


def cost():
    return pl.CostEstimate(flops=1, bytes_accessed=1, transcendentals=0)


def swap(x, axis, stride):
    size = lax.axis_size(axis)
    return lax.ppermute(x, axis, [(i, i ^ stride) for i in range(size)])


def halving(size, last):
    strides = []
    step = size // 2
    while step >= last:
        strides.append(step)
        step //= 2
    return strides


def offsets(strides):
    order = [0]
    for stride in strides:
        order = order + [o ^ stride for o in order]
    return order


def after(value, token):
    return lax.optimization_barrier((value, token))[0]


def dot(a, b):
    return jnp.dot(a, b, preferred_element_type=F32)


def dot_t(a, b):
    return lax.dot_general(a, b, (((1,), (1,)), ((), ())), preferred_element_type=F32)


def norm_body(depth, own_rel, meta, hidden, gain, own, sent, scratch):
    rows = hidden[...].astype(F32)
    centered = rows - jnp.mean(rows, axis=-1, keepdims=True)
    spread = jnp.mean(centered * centered, axis=-1, keepdims=True)
    scratch[...] = (centered * lax.rsqrt(spread + EPSILON) * gain[...]).astype(BF16)
    me = meta[0]
    for e, rel in enumerate(own_rel):
        start = pl.multiple_of((me ^ rel) * depth, 128)
        own[e] = scratch[:, pl.ds(start, depth)]
        start = pl.multiple_of((me ^ rel ^ 1) * depth, 128)
        sent[e] = scratch[:, pl.ds(start, depth)]


def norm_call(meta, hidden, gain, depth, own_rel):
    rows, width = hidden.shape
    shape = jax.ShapeDtypeStruct((len(own_rel), rows, depth), BF16)
    return pl.pallas_call(
        lambda *refs: norm_body(depth, own_rel, *refs),
        out_shape=(shape, shape),
        in_specs=[
            pl.BlockSpec(memory_space=SMEM),
            pl.BlockSpec(memory_space=pltpu.VMEM),
            pl.BlockSpec(memory_space=pltpu.VMEM),
        ],
        out_specs=(pl.BlockSpec(memory_space=pltpu.VMEM), pl.BlockSpec(memory_space=pltpu.VMEM)),
        scratch_shapes=[pltpu.VMEM((rows, width), BF16)],
        compiler_params=params(),
        cost_estimate=cost(),
        name="layer_norm",
    )(meta, hidden, gain)


def load_weights(hg, refs):
    weights = []
    for ref in refs:
        blocks = [ref[0, hg ^ q] for q in range(ref.shape[1])]
        weights.append(jnp.concatenate(blocks, axis=0))
    return weights


def product(xs, ws):
    total = None
    k = 0
    for x in xs:
        for e in range(x.shape[0]):
            part = x[e]
            part = part.reshape(-1, part.shape[-1])
            term = dot(part, ws[k])
            total = term if total is None else total + term
            k += 1
    return total


def whole(x):
    nd = len(x.shape)
    return pl.BlockSpec(x.shape, lambda *_: (0,) * nd)


def by_step(x, first=0):
    nd = len(x.shape) - 1
    return pl.BlockSpec((1,) + tuple(x.shape[1:]), lambda i, *_: (first + i,) + (0,) * nd)


def weight_specs(ws):
    return [by_step(w) for w in ws]


def partner_body(streams, count, meta, *refs):
    xs, ws, out = refs[: 2 * streams], refs[2 * streams : 2 * streams + count], refs[-1]
    ws = load_weights(meta[2], ws)
    half = out.shape[1] // 2
    for core in (0, 1):
        out[0, core * half : (core + 1) * half] = product(xs[core * streams : (core + 1) * streams], ws).astype(BF16)


def partner_call(meta, xs, ws, rows, heads):
    streams = len(xs) // 2
    width = ws[0].shape[-1]
    out = jax.ShapeDtypeStruct((heads, rows, width), BF16)
    return pl.pallas_call(
        lambda *refs: partner_body(streams, len(ws), *refs),
        out_shape=out,
        grid_spec=pltpu.PrefetchScalarGridSpec(
            num_scalar_prefetch=1,
            grid=(heads,),
            in_specs=[whole(x) for x in xs] + weight_specs(ws),
            out_specs=by_step(out),
        ),
        compiler_params=params(),
        cost_estimate=cost(),
        name="partner_product",
    )(meta, *xs, *ws)


def finish_body(streams, count, cap, order_h, order_t, meta, lengths, owners, *refs):
    xs, ws = refs[: 2 * streams], refs[2 * streams : 2 * streams + count]
    arrived, cosine, sine, cache, query, kv = refs[2 * streams + count : 2 * streams + count + 6]
    placed, total, slots, counts = refs[-4:]
    me, tp, hg = meta[0], meta[1], meta[2]
    ws = load_weights(hg, ws)
    half = total.shape[0] // 2
    for core in (0, 1):
        rows = slice(core * half, (core + 1) * half)
        total[rows] = product(xs[core * streams : (core + 1) * streams], ws) + arrived[0, rows].astype(F32)
    hd = query.shape[2]
    nt = len(order_t)
    run_rows = total.shape[0] // (len(order_h) * nt)
    lane = lax.broadcasted_iota(jnp.int32, (run_rows, hd), 1)
    half_rot = ROT // 2
    m = 0
    for rel_h in order_h:
        for rel_t in order_t:
            start = pl.multiple_of(((hg ^ rel_h) * nt + (tp ^ rel_t)) * run_rows, run_rows)
            rows = slice(m * run_rows, (m + 1) * run_rows)
            cos_rows, sin_rows = cosine[pl.ds(start, run_rows)], sine[pl.ds(start, run_rows)]

            def rotated(part):
                other = jnp.where(
                    lane < half_rot, pltpu.roll(part, hd - half_rot, 1), pltpu.roll(part, half_rot, 1)
                )
                return (part * cos_rows + other * sin_rows).astype(BF16)

            query[0, pl.ds(start, run_rows)] = rotated(total[rows, :hd])
            kv[0, pl.ds(start, run_rows), :hd] = rotated(total[rows, hd : 2 * hd])
            kv[0, pl.ds(start, run_rows), hd:] = total[rows, 2 * hd :].astype(BF16)
            m += 1
    owner_count = placed.shape[0]
    blocks = owners.shape[1]
    cached_blocks = lengths[me] // BLOCK
    valid_end = cached_blocks + query.shape[1] // BLOCK
    for s in range(owner_count * cap):
        slots[s] = -1
    for o in range(owner_count):
        counts[o] = 0
    for b in range(blocks):

        @pl.when(b < valid_end)
        def _():
            owner = owners[me, b]
            rank = counts[owner]

            @pl.when(rank < cap)
            def _():
                slots[owner * cap + rank] = b

            counts[owner] = rank + 1

    for s in range(owner_count * cap):
        block = slots[s]
        o, c = divmod(s, cap)

        @pl.when(block < 0)
        def _():
            placed[o, 0, c] = jnp.zeros(placed.shape[3:], BF16)

        @pl.when((block >= 0) & (block < cached_blocks))
        def _():
            at = pl.multiple_of(block * BLOCK, BLOCK)
            placed[o, 0, c] = cache[0, 0, pl.ds(at, BLOCK)]

        @pl.when(block >= cached_blocks)
        def _():
            at = pl.multiple_of((block - cached_blocks) * BLOCK, BLOCK)
            placed[o, 0, c] = kv[0, pl.ds(at, BLOCK)]


def cache_by_step(cache, first):
    return pl.BlockSpec((1, 1) + cache.shape[2:], lambda i, meta, *_: (0, meta[3] + first + i, 0, 0))


def finish_call(meta, lengths, owners, xs, ws, arrived, cosine, sine, cache, first, cap, owner_count, order_h, order_t):
    streams = len(xs) // 2
    heads, rows, width = arrived.shape
    hd = width // 3
    cache_spec = cache_by_step(cache, first)
    outs = [(heads, rows, hd), (heads, rows, 2 * hd), (owner_count, heads, cap, BLOCK, 2 * hd)]
    outs = tuple(jax.ShapeDtypeStruct(o, BF16) for o in outs)
    placed_spec = pl.BlockSpec((owner_count, 1, cap, BLOCK, 2 * hd), lambda i, *_: (0, i, 0, 0, 0))
    return pl.pallas_call(
        lambda *refs: finish_body(streams, len(ws), cap, order_h, order_t, *refs),
        out_shape=outs,
        grid_spec=pltpu.PrefetchScalarGridSpec(
            num_scalar_prefetch=3,
            grid=(heads,),
            in_specs=[whole(x) for x in xs]
            + weight_specs(ws)
            + [by_step(arrived), whole(cosine), whole(sine), cache_spec],
            out_specs=(by_step(outs[0]), by_step(outs[1]), placed_spec),
            scratch_shapes=[
                pltpu.VMEM((rows, width), F32),
                pltpu.SMEM((owner_count * cap,), jnp.int32),
                pltpu.SMEM((owner_count,), jnp.int32),
            ],
        ),
        compiler_params=params(),
        cost_estimate=cost(),
        name="finish_projection",
    )(meta, lengths, owners, *xs, *ws, arrived, cosine, sine, cache)


def attend_body(q_rows, meta, lengths, query, kv, cache, out):
    hd = query.shape[2]
    length = lengths[meta[0]]
    factor = math.log2(math.e) / math.sqrt(hd)
    old_col = lax.broadcasted_iota(jnp.int32, (q_rows, cache.shape[2]), 1)
    causal = lax.broadcasted_iota(jnp.int32, (q_rows, q_rows), 1) <= lax.broadcasted_iota(
        jnp.int32, (q_rows, q_rows), 0
    )
    for step in range(query.shape[1] // q_rows):
        first = step * q_rows
        q = query[0, first : first + q_rows]
        old = jnp.where(old_col < length, dot_t(q, cache[0, 0, :, :hd]), -jnp.inf)
        diag = jnp.where(causal, dot_t(q, kv[0, first : first + q_rows, :hd]), -jnp.inf)
        top = jnp.maximum(jnp.max(old, axis=1, keepdims=True), jnp.max(diag, axis=1, keepdims=True))
        if step:
            new = dot_t(q, kv[0, :first, :hd])
            top = jnp.maximum(top, jnp.max(new, axis=1, keepdims=True))
        old = jnp.exp2((old - top) * factor)
        diag = jnp.exp2((diag - top) * factor)
        total = jnp.sum(old, axis=1, keepdims=True) + jnp.sum(diag, axis=1, keepdims=True)
        result = dot(old.astype(BF16), cache[0, 0, :, hd:]) + dot(diag.astype(BF16), kv[0, first : first + q_rows, hd:])
        if step:
            new = jnp.exp2((new - top) * factor)
            total = total + jnp.sum(new, axis=1, keepdims=True)
            result = result + dot(new.astype(BF16), kv[0, :first, hd:])
        out[0, first : first + q_rows] = (result / total).astype(BF16)


def attend_call(meta, lengths, query, kv, cache, first, q_rows=256):
    heads, rows, hd = query.shape
    out = jax.ShapeDtypeStruct((heads, rows, hd), BF16)
    return pl.pallas_call(
        lambda *refs: attend_body(q_rows, *refs),
        out_shape=out,
        grid_spec=pltpu.PrefetchScalarGridSpec(
            num_scalar_prefetch=2,
            grid=(heads,),
            in_specs=[by_step(query), by_step(kv), cache_by_step(cache, first)],
            out_specs=by_step(out),
        ),
        compiler_params=params(),
        cost_estimate=cost(),
        name="attention",
    )(meta, lengths, query, kv, cache)


def split_body(order_t, meta, *refs):
    held, outs = refs[: -len(order_t)], refs[-len(order_t) :]
    cols = outs[0].shape[-1]
    for r, out in zip(order_t, outs):
        start = pl.multiple_of((meta[1] ^ r) * cols, cols)
        for d, ref in enumerate(held):
            out[d] = ref[:, :, pl.ds(start, cols)]


def split_call(meta, held, order_t):
    heads, hd, width = held[0].shape
    cols = width // len(order_t)
    if cols % 128:
        stacked = jnp.stack(held).reshape(len(held), heads, hd, len(order_t), cols)
        return [lax.dynamic_index_in_dim(stacked, meta[1] ^ r, 3, keepdims=False) for r in order_t]
    vmem = pl.BlockSpec(memory_space=pltpu.VMEM)
    return pl.pallas_call(
        lambda *refs: split_body(order_t, *refs),
        out_shape=[jax.ShapeDtypeStruct((len(held), heads, hd, cols), BF16) for _ in order_t],
        in_specs=[pl.BlockSpec(memory_space=SMEM)] + [vmem] * len(held),
        out_specs=[vmem] * len(order_t),
        compiler_params=params(),
        cost_estimate=cost(),
        name="split_columns",
    )(meta, *held)


def output_body(first, heads, group, order_h, order_t, with_sum, meta, *refs):
    parts, weights = refs[: 2 * heads], refs[2 * heads : 2 * heads + len(order_t)]
    out = refs[-1]
    hg = meta[2]
    dps = weights[0].shape[0]
    total = refs[-2][...] if with_sum else None
    for j in range(heads):
        left, right = [], []
        for i, rel_h in enumerate(order_h):
            core, h = divmod(i, len(order_h) // 2)
            for t in range(len(order_t)):
                left.append(parts[2 * j + core][h, t])
                head = (hg ^ rel_h) * group + first + j
                right.append(jnp.concatenate([weights[t][meta[4 + d], head] for d in range(dps)], axis=1))
        term = dot(jnp.concatenate(left, axis=1), jnp.concatenate(right, axis=0))
        total = term if total is None else total + term
    out[...] = total.astype(out.dtype)


def output_call(meta, parts, weights, rows, first, group, order_h, order_t, total=None, dtype=F32):
    dps, _, _, cols = weights[0].shape
    vmem = pl.BlockSpec(memory_space=pltpu.VMEM)
    operands = (meta, *parts, *weights) + (() if total is None else (total,))
    return pl.pallas_call(
        lambda *refs: output_body(first, len(parts) // 2, group, order_h, order_t, total is not None, *refs),
        out_shape=jax.ShapeDtypeStruct((rows, dps * cols), dtype),
        in_specs=[pl.BlockSpec(memory_space=SMEM)] + [vmem] * (len(operands) - 1),
        out_specs=vmem,
        compiler_params=params(),
        cost_estimate=cost(),
        name="output_projection",
    )(*operands)


def output_plain(meta, tp, hg, parts, weights, rows, group, order_h, order_t):
    del tp
    dps, heads, hd, cols = weights[0].shape
    stacked = jnp.stack(weights).reshape(len(order_t), dps, len(order_h), group, hd, cols)
    stacked = jnp.take(stacked, meta[4 : 4 + dps], axis=1)
    stacked = jnp.take(stacked, hg ^ jnp.array(order_h, jnp.int32), axis=2)
    total = None
    for j in range(group):
        left = jnp.concatenate([parts[2 * j], parts[2 * j + 1]], axis=0)
        left = left.transpose(2, 0, 1, 3).reshape(rows, -1)
        right = stacked[:, :, :, j].transpose(2, 0, 3, 1, 4).reshape(-1, dps * cols)
        term = dot(left, right)
        total = term if total is None else total + term
    return total.astype(BF16)


def collect_body(*refs):
    head = 0
    for piece in refs[:-1]:
        for j in range(piece.shape[1]):
            refs[-1][0, head, 0] = piece[0, j]
            head += 1


def collect_call(pieces):
    heads = sum(p.shape[1] for p in pieces)
    requests = pieces[0].shape[0]
    tail = pieces[0].shape[2:]
    return pl.pallas_call(
        collect_body,
        grid=(requests,),
        out_shape=jax.ShapeDtypeStruct((1, heads, requests) + tail, BF16),
        in_specs=[by_step(p) for p in pieces],
        out_specs=pl.BlockSpec((1, heads, 1) + tail, lambda r: (0, 0, r, 0, 0, 0)),
        compiler_params=params(),
        cost_estimate=cost(),
        name="collect_blocks",
    )(*pieces)


def residual_body(nd, hidden, summed, out):
    members, _, columns = summed.shape
    cols = columns // nd
    for d in range(nd):
        for m in range(members):
            at = slice((d * members + m) * cols, (d * members + m + 1) * cols)
            out[:, at] = (hidden[:, at].astype(F32) + summed[m, :, d * cols : (d + 1) * cols].astype(F32)).astype(BF16)


def residual_call(hidden, summed, nd):
    vmem = pl.BlockSpec(memory_space=pltpu.VMEM)
    return pl.pallas_call(
        lambda *refs: residual_body(nd, *refs),
        out_shape=jax.ShapeDtypeStruct(hidden.shape, BF16),
        in_specs=[vmem, vmem],
        out_specs=vmem,
        compiler_params=params(),
        cost_estimate=cost(),
        name="residual",
    )(hidden, summed)


def plane_gather(x, dim_h, dim_t, h_strides, t_strides, h_first, token=None):
    def over_h(x):
        for s in h_strides[:-1]:
            x = jnp.concatenate([x, swap(x, "hg", s)], axis=dim_h)
        return x

    def over_t(x):
        for s in t_strides:
            x = jnp.concatenate([x, swap(x, "tp", s)], axis=dim_t)
        return x

    x = over_t(over_h(x)) if h_first else over_h(over_t(x))
    if token is not None:
        x = after(x, token)
    return x, swap(x, "hg", h_strides[-1])


def head_gather(attended, h_strides, t_strides, token=None):
    parts = []
    for j in range(attended.shape[0]):
        parts += plane_gather(attended[j][None, None], 0, 1, h_strides, t_strides, j % 2 == 0, token)
    return parts


def chunks_of(group):
    return [group // 2, group - group // 2] if group > 1 else [1]


def on_device(hidden_in, norm_gain, qkv_weight, out_weight, cache_kv, cached_lengths, owner_table):
    nt, nh, nd = lax.axis_size("tp"), lax.axis_size("hg"), lax.axis_size("dp")
    tp, hg, dp = lax.axis_index("tp"), lax.axis_index("hg"), lax.axis_index("dp")
    local_rows, width = hidden_in.shape[2:]
    local_depth, _, local_heads, hd = qkv_weight.shape
    group = local_heads // nh
    depth = local_depth * nh
    rows = local_rows * nt * nh
    cap = (cache_kv.shape[2] + rows) // BLOCK // nd
    length = lax.dynamic_index_in_dim(cached_lengths, dp, 0, keepdims=False)

    far, all_d = halving(nd, 2), halving(nd, 1)
    own_rel = offsets(far)
    h_strides, t_strides = halving(nh, 1), halving(nt, 1)
    order_h, order_t = offsets(h_strides), offsets(t_strides)
    members = dp ^ jnp.arange(nd, dtype=jnp.int32)
    place = sum(jnp.where(members == rel, k, 0) for k, rel in enumerate(offsets(all_d))).astype(jnp.int32)
    meta = jnp.concatenate([jnp.stack([dp, tp, hg, hg * group]).astype(jnp.int32), place])

    out_held = [out_weight]
    for s in far:
        out_held = out_held + [swap(w, "dp", s) for w in out_held]
    out_near = [swap(out_weight, "dp", 1)]
    by_head = qkv_weight.reshape(local_depth, 3, nh, group, hd).transpose(2, 3, 0, 1, 4)
    by_head = by_head.reshape(nh, group, local_depth, 3 * hd)
    given = [lax.dynamic_index_in_dim(by_head, hg ^ s, 0, keepdims=False) for s in range(nh)]
    own, sent = norm_call(meta, hidden_in[0, 0], norm_gain.reshape(1, width), depth, own_rel)
    sent = swap(sent, "dp", 1)

    positions = length + jnp.arange(rows, dtype=jnp.int32)
    half_rot = ROT // 2
    frequency = 10000.0 ** (-2.0 * jnp.arange(half_rot, dtype=F32) / ROT)
    angles = positions.astype(F32)[:, None] * frequency[None, :]
    cos_half, sin_half = jnp.cos(angles), jnp.sin(angles)
    cosine = jnp.concatenate([cos_half, cos_half, jnp.ones((rows, hd - ROT), F32)], axis=1)
    sine = jnp.concatenate([-sin_half, sin_half, jnp.zeros((rows, hd - ROT), F32)], axis=1)
    sizes = chunks_of(group)
    firsts = [sum(sizes[:c]) for c in range(len(sizes))]
    mine = []
    for f, size in zip(firsts, sizes):
        parts = [piece[f : f + size] for piece in given]
        mine.append(jnp.stack([swap(p, "hg", s) if s else p for s, p in enumerate(parts)], axis=1))

    live = dict(out=out_held, near=out_near, mine=mine, x=(own, sent), tables=(cosine, sine))
    live = lax.optimization_barrier(live)

    cols = out_weight.shape[2] // nt
    weights, arrived, gathered, handed = [], [], [], []
    chunks = len(sizes)
    for stage in range(1, chunks + 3):
        c = stage - 1
        if c < chunks:
            held = [live["mine"][c]]
            for s in far:
                held = held + [swap(w, "dp", s) for w in held]
            weights.append(held)
        if stage == 1:
            cut = len(own_rel) // 2
            for name, x in zip(("own", "pair"), live.pop("x")):
                x = x[:, None, None]
                streams = [
                    plane_gather(x[:cut], 1, 2, h_strides, t_strides, True),
                    plane_gather(x[cut:], 1, 2, h_strides, t_strides, False),
                ]
                live[name] = [s[0] for s in streams] + [s[1] for s in streams]
            live["near"] = live["near"] + [swap(w, "dp", 1) for w in live["out"][1:]]
        if stage == 2:
            held = split_call(meta, live.pop("out") + live.pop("near"), order_t)
            live["out_weights"] = [swap(w, "tp", r) if r else w for w, r in zip(held, order_t)]
        if "attended" in live:
            gathered.append(head_gather(live["attended"], h_strides, t_strides))
        c = stage - 3
        if 0 <= c < chunks:
            query, kv, placed = finish_call(
                meta, cached_lengths, owner_table, live["own"], live["weights"][c], live["arrived"][c],
                *live["tables"], cache_kv, firsts[c], cap, nd, order_h, order_t,
            )
            handed.append(lax.all_to_all(placed, "dp", 0, 0, tiled=True))
            live["attended"] = attend_call(meta, cached_lengths, query, kv, cache_kv, firsts[c])
        c = stage - 2
        if 0 <= c < chunks:
            partial = partner_call(meta, live["pair"], live["weights"][c], rows, sizes[c])
            arrived.append(swap(partial, "dp", 1))
        if stage == chunks + 2:
            break
        live.update(weights=weights, arrived=arrived, handed=handed, gathered=gathered)
        live = lax.optimization_barrier(live)
        weights, arrived, handed, gathered = (list(live[k]) for k in ("weights", "arrived", "handed", "gathered"))
    out_weights = live["out_weights"]
    attended = live["attended"]
    if cols % 128 == 0:
        summed = None
        for c, parts in enumerate(gathered):
            summed = output_call(meta, parts, out_weights, rows, firsts[c], group, order_h, order_t, summed)
        parts = head_gather(attended, h_strides, t_strides, summed)
        summed = output_call(meta, parts, out_weights, rows, firsts[-1], group, order_h, order_t, summed, BF16)
    else:
        gathered.append(head_gather(attended, h_strides, t_strides))
        parts = [p for parts in gathered for p in parts]
        summed = output_plain(meta, tp, hg, parts, out_weights, rows, group, order_h, order_t)
    summed = after(summed, handed[-1])
    summed = lax.all_to_all(
        summed.reshape(nh * nt, local_rows, nd * cols), ("hg", "tp"), 0, 0, tiled=True
    )
    if cols % 128 == 0:
        hidden_out = residual_call(hidden_in[0, 0], summed, nd)
    else:
        summed = summed.reshape(nh, nt, local_rows, nd, cols).transpose(2, 3, 0, 1, 4).reshape(local_rows, width)
        hidden_out = (hidden_in[0, 0].astype(F32) + summed.astype(F32)).astype(BF16)
    return hidden_out[None, None], collect_call(handed)


def solution(mesh):
    return jax.shard_map(
        on_device,
        mesh=mesh,
        in_specs=(
            P("dp", "hg", "tp", None),
            P(),
            P(("dp", "hg"), None, "tp", None),
            P("tp", None, ("dp", "hg")),
            P("dp", "tp", None, None),
            P(),
            P(),
        ),
        out_specs=(P("dp", "hg", "tp", None), P("dp", ("tp", "hg"), None, None, None, None)),
        check_vma=False,
    )
```

```python
import math

import jax
import jax.numpy as jnp
from jax import lax
from jax.experimental import pallas as pl
from jax.experimental.pallas import tpu as pltpu
from jax.sharding import PartitionSpec as P

ROT = 32
BLOCK = 128
EPSILON = 1e-05
VMEM_LIMIT = 48 * 1024 * 1024

SMEM = pltpu.SMEM
BF16 = jnp.bfloat16
F32 = jnp.float32


def params():
    return pltpu.CompilerParams(vmem_limit_bytes=VMEM_LIMIT)


def cost():
    return pl.CostEstimate(flops=1, bytes_accessed=1, transcendentals=0)


def hold(xs, microseconds):
    hbm = pl.BlockSpec(memory_space=pl.ANY)
    held = pl.pallas_call(
        lambda *refs: None,
        out_shape=[jax.ShapeDtypeStruct(x.shape, x.dtype) for x in xs],
        in_specs=[hbm] * len(xs),
        out_specs=[hbm] * len(xs),
        input_output_aliases={i: i for i in range(len(xs))},
        cost_estimate=pl.CostEstimate(flops=int(microseconds * 1e9), bytes_accessed=1, transcendentals=0),
        name="hold",
    )(*xs)
    return list(held)


def swap(x, axis, stride):
    size = lax.axis_size(axis)
    return lax.ppermute(x, axis, [(i, i ^ stride) for i in range(size)])


def halving(size, last):
    strides = []
    step = size // 2
    while step >= last:
        strides.append(step)
        step //= 2
    return strides


def offsets(strides):
    order = [0]
    for stride in strides:
        order = order + [o ^ stride for o in order]
    return order


def after(value, token):
    return lax.optimization_barrier((value, token))[0]


def dot(a, b):
    return jnp.dot(a, b, preferred_element_type=F32)


def dot_t(a, b):
    return lax.dot_general(a, b, (((1,), (1,)), ((), ())), preferred_element_type=F32)


def norm_body(depth, own_rel, meta, hidden, gain, own, sent, scratch):
    rows = hidden[...].astype(F32)
    centered = rows - jnp.mean(rows, axis=-1, keepdims=True)
    spread = jnp.mean(centered * centered, axis=-1, keepdims=True)
    scratch[...] = (centered * lax.rsqrt(spread + EPSILON) * gain[...]).astype(BF16)
    me = meta[0]
    for e, rel in enumerate(own_rel):
        start = pl.multiple_of((me ^ rel) * depth, 128)
        own[e] = scratch[:, pl.ds(start, depth)]
        start = pl.multiple_of((me ^ rel ^ 1) * depth, 128)
        sent[e] = scratch[:, pl.ds(start, depth)]


def norm_call(meta, hidden, gain, depth, own_rel):
    rows, width = hidden.shape
    shape = jax.ShapeDtypeStruct((len(own_rel), rows, depth), BF16)
    return pl.pallas_call(
        lambda *refs: norm_body(depth, own_rel, *refs),
        out_shape=(shape, shape),
        in_specs=[
            pl.BlockSpec(memory_space=SMEM),
            pl.BlockSpec(memory_space=pltpu.VMEM),
            pl.BlockSpec(memory_space=pltpu.VMEM),
        ],
        out_specs=(pl.BlockSpec(memory_space=pltpu.VMEM), pl.BlockSpec(memory_space=pltpu.VMEM)),
        scratch_shapes=[pltpu.VMEM((rows, width), BF16)],
        compiler_params=params(),
        cost_estimate=cost(),
        name="layer_norm",
    )(meta, hidden, gain)


def load_weights(refs):
    return [ref[:, 0].reshape(-1, ref.shape[-1]) for ref in refs]


def product(xs, ws, total):
    half = total.shape[0] // 2
    streams = len(xs) // 2
    for core in (0, 1):
        result = None
        k = 0
        for x in xs[core * streams : (core + 1) * streams]:
            for e in range(x.shape[0]):
                term = dot(x[e].reshape(-1, x.shape[-1]), ws[k])
                result = term if result is None else result + term
                k += 1
        total[core * half : (core + 1) * half] = result.astype(total.dtype)


def whole(x):
    nd = len(x.shape)
    return pl.BlockSpec(x.shape, lambda *_: (0,) * nd)


def by_step(x, first=0):
    nd = len(x.shape) - 1
    return pl.BlockSpec((1,) + tuple(x.shape[1:]), lambda i, *_: (first + i,) + (0,) * nd)


def weight_specs(ws, first):
    return [pl.BlockSpec((w.shape[0], 1) + w.shape[2:], lambda i, *_: (0, first + i, 0, 0)) for w in ws]


def partner_body(inputs, *refs):
    product(refs[:inputs], load_weights(refs[inputs:-1]), refs[-1].at[0])


def partner_call(xs, ws, rows, at, heads=1):
    out = jax.ShapeDtypeStruct((heads, rows, ws[0].shape[-1]), BF16)
    return pl.pallas_call(
        lambda *refs: partner_body(len(xs), *refs),
        grid=(heads,),
        out_shape=out,
        in_specs=[whole(x) for x in xs] + weight_specs(ws, at),
        out_specs=by_step(out),
        compiler_params=params(),
        cost_estimate=cost(),
        name="partner_product",
    )(*xs, *ws)


def finish_body(inputs, cap, order_h, order_t, meta, lengths, owners, *refs):
    xs, ws = refs[:inputs], load_weights(refs[inputs:-10])
    arrived, cosine, sine, cache, query, kv, placed, total, slots, counts = refs[-10:]
    me, tp, hg = meta[0], meta[1], meta[2]
    product(xs, ws, total)
    hd = query.shape[2]
    members = [(h, t) for h in order_h for t in order_t]
    run_rows = total.shape[0] // len(members)
    lane = lax.broadcasted_iota(jnp.int32, (run_rows, hd), 1)
    half_rot = ROT // 2
    for m, (rel_h, rel_t) in enumerate(members):
        rows = slice(m * run_rows, (m + 1) * run_rows)
        start = pl.multiple_of(((hg ^ rel_h) * len(order_t) + (tp ^ rel_t)) * run_rows, run_rows)
        to = pl.ds(start, run_rows)
        cos_rows, sin_rows = cosine[to], sine[to]

        def summed(low):
            return total[rows, low : low + hd] + arrived[0, rows, low : low + hd].astype(F32)

        def rotated(part):
            other = jnp.where(
                lane < half_rot, pltpu.roll(part, hd - half_rot, 1), pltpu.roll(part, half_rot, 1)
            )
            return (part * cos_rows + other * sin_rows).astype(BF16)

        query[0, to] = rotated(summed(0))
        kv[0, to, :hd] = rotated(summed(hd))
        kv[0, to, hd:] = summed(2 * hd).astype(BF16)
    owner_count = placed.shape[0]
    blocks = owners.shape[1]
    cached_blocks = lengths[me] // BLOCK
    valid_end = cached_blocks + query.shape[1] // BLOCK
    for s in range(owner_count * cap):
        slots[s] = -1
    for o in range(owner_count):
        counts[o] = 0
    for b in range(blocks):

        @pl.when(b < valid_end)
        def _():
            owner = owners[me, b]
            rank = counts[owner]

            @pl.when(rank < cap)
            def _():
                slots[owner * cap + rank] = b

            counts[owner] = rank + 1

    for s in range(owner_count * cap):
        block = slots[s]
        o, c = divmod(s, cap)

        @pl.when(block < 0)
        def _():
            placed[o, 0, c] = jnp.zeros(placed.shape[3:], BF16)

        @pl.when((block >= 0) & (block < cached_blocks))
        def _():
            at = pl.multiple_of(block * BLOCK, BLOCK)
            placed[o, 0, c] = cache[0, 0, pl.ds(at, BLOCK)]

        @pl.when(block >= cached_blocks)
        def _():
            at = pl.multiple_of((block - cached_blocks) * BLOCK, BLOCK)
            placed[o, 0, c] = kv[0, pl.ds(at, BLOCK)]


def cache_by_step(cache, first):
    return pl.BlockSpec((1, 1) + cache.shape[2:], lambda i, meta, *_: (0, meta[3] + first + i, 0, 0))


def finish_call(meta, lengths, owners, xs, ws, arrived, cosine, sine, cache, at, first, cap, owner_count, orders):
    heads, rows, width = arrived.shape
    hd = width // 3
    cache_spec = cache_by_step(cache, first)
    outs = [(heads, rows, hd), (heads, rows, 2 * hd), (owner_count, heads, cap, BLOCK, 2 * hd)]
    outs = tuple(jax.ShapeDtypeStruct(o, BF16) for o in outs)
    placed_spec = pl.BlockSpec((owner_count, 1, cap, BLOCK, 2 * hd), lambda i, *_: (0, i, 0, 0, 0))
    return pl.pallas_call(
        lambda *refs: finish_body(len(xs), cap, *orders, *refs),
        out_shape=outs,
        grid_spec=pltpu.PrefetchScalarGridSpec(
            num_scalar_prefetch=3,
            grid=(heads,),
            in_specs=[whole(x) for x in xs]
            + weight_specs(ws, at)
            + [by_step(arrived), whole(cosine), whole(sine), cache_spec],
            out_specs=(by_step(outs[0]), by_step(outs[1]), placed_spec),
            scratch_shapes=[
                pltpu.VMEM((rows, width), F32),
                pltpu.SMEM((owner_count * cap,), jnp.int32),
                pltpu.SMEM((owner_count,), jnp.int32),
            ],
        ),
        compiler_params=params(),
        cost_estimate=cost(),
        name="finish_projection",
    )(meta, lengths, owners, *xs, *ws, arrived, cosine, sine, cache)


def attend_body(q_rows, meta, lengths, query, kv, cache, out):
    hd = query.shape[2]
    length = lengths[meta[0]]
    factor = math.log2(math.e) / math.sqrt(hd)
    old_col = lax.broadcasted_iota(jnp.int32, (q_rows, cache.shape[2]), 1)
    causal = lax.broadcasted_iota(jnp.int32, (q_rows, q_rows), 1) <= lax.broadcasted_iota(
        jnp.int32, (q_rows, q_rows), 0
    )
    for step in range(query.shape[1] // q_rows):
        first = step * q_rows
        q = query[0, first : first + q_rows]
        old = jnp.where(old_col < length, dot_t(q, cache[0, 0, :, :hd]), -jnp.inf)
        diag = jnp.where(causal, dot_t(q, kv[0, first : first + q_rows, :hd]), -jnp.inf)
        top = jnp.maximum(jnp.max(old, axis=1, keepdims=True), jnp.max(diag, axis=1, keepdims=True))
        if step:
            new = dot_t(q, kv[0, :first, :hd])
            top = jnp.maximum(top, jnp.max(new, axis=1, keepdims=True))
        old = jnp.exp2((old - top) * factor)
        diag = jnp.exp2((diag - top) * factor)
        total = jnp.sum(old, axis=1, keepdims=True) + jnp.sum(diag, axis=1, keepdims=True)
        result = dot(old.astype(BF16), cache[0, 0, :, hd:]) + dot(diag.astype(BF16), kv[0, first : first + q_rows, hd:])
        if step:
            new = jnp.exp2((new - top) * factor)
            total = total + jnp.sum(new, axis=1, keepdims=True)
            result = result + dot(new.astype(BF16), kv[0, :first, hd:])
        out[0, first : first + q_rows] = (result / total).astype(BF16)


def attend_call(meta, lengths, query, kv, cache, first, q_rows=256):
    heads, rows, hd = query.shape
    out = jax.ShapeDtypeStruct((heads, rows, hd), BF16)
    return pl.pallas_call(
        lambda *refs: attend_body(q_rows, *refs),
        out_shape=out,
        grid_spec=pltpu.PrefetchScalarGridSpec(
            num_scalar_prefetch=2,
            grid=(heads,),
            in_specs=[by_step(query), by_step(kv), cache_by_step(cache, first)],
            out_specs=by_step(out),
        ),
        compiler_params=params(),
        cost_estimate=cost(),
        name="attention",
    )(meta, lengths, query, kv, cache)


def split_body(order_t, meta, *refs):
    held, outs = refs[: -len(order_t)], refs[-len(order_t) :]
    cols = outs[0].shape[-1]
    for r, out in zip(order_t, outs):
        start = pl.multiple_of((meta[1] ^ r) * cols, cols)
        for d, ref in enumerate(held):
            out[d] = ref[:, :, pl.ds(start, cols)]


def split_call(meta, held, order_t):
    heads, hd, width = held[0].shape
    cols = width // len(order_t)
    if cols % 128:
        stacked = jnp.stack(held).reshape(len(held), heads, hd, len(order_t), cols)
        return [lax.dynamic_index_in_dim(stacked, meta[1] ^ r, 3, keepdims=False) for r in order_t]
    vmem = pl.BlockSpec(memory_space=pltpu.VMEM)
    return pl.pallas_call(
        lambda *refs: split_body(order_t, *refs),
        out_shape=[jax.ShapeDtypeStruct((len(held), heads, hd, cols), BF16) for _ in order_t],
        in_specs=[pl.BlockSpec(memory_space=SMEM)] + [vmem] * len(held),
        out_specs=[vmem] * len(order_t),
        compiler_params=params(),
        cost_estimate=cost(),
        name="split_columns",
    )(meta, *held)


def output_body(first, heads, group, order_h, order_t, with_sum, spread, meta, *refs):
    pieces = len(order_h) * len(order_t)
    parts, weights = refs[: 2 * heads], refs[2 * heads : 2 * heads + len(order_t)]
    rest = refs[2 * heads + len(order_t) :]
    tp, hg = meta[1], meta[2]
    total = rest[0][...] if with_sum else None
    for j in range(heads):
        left, right = [], []
        for i, rel_h in enumerate(order_h):
            core, h = divmod(i, len(order_h) // 2)
            for t in range(len(order_t)):
                left.append(parts[2 * j + core][h, t])
                head = (hg ^ rel_h) * group + first + j
                right.append(jnp.concatenate([weights[t][d, head] for d in range(weights[t].shape[0])], axis=1))
        term = dot(jnp.concatenate(left, axis=1), jnp.concatenate(right, axis=0))
        total = term if total is None else total + term
    if not spread:
        rest[-1][...] = total
        return
    scratch, outs = rest[-1], rest[-1 - pieces : -1]
    scratch[...] = total
    run_rows = outs[0].shape[0]
    for i, rel_h in enumerate(order_h):
        for t, rel_t in enumerate(order_t):
            start = pl.multiple_of(((hg ^ rel_h) * len(order_t) + (tp ^ rel_t)) * run_rows, run_rows)
            outs[i * len(order_t) + t][...] = scratch[pl.ds(start, run_rows)].astype(BF16)


def output_call(meta, parts, weights, rows, first, group, order_h, order_t, total=None, spread=False):
    members = len(order_h) * len(order_t)
    dps, cols = weights[0].shape[0], weights[0].shape[-1]
    vmem = pl.BlockSpec(memory_space=pltpu.VMEM)
    operands = (meta, *parts, *weights) + (() if total is None else (total,))
    heads = len(parts) // 2
    out = jax.ShapeDtypeStruct((rows, dps * cols), F32)
    piece = jax.ShapeDtypeStruct((rows // members, dps * cols), BF16)
    return pl.pallas_call(
        lambda *refs: output_body(first, heads, group, order_h, order_t, total is not None, spread, *refs),
        out_shape=[piece] * members if spread else out,
        in_specs=[pl.BlockSpec(memory_space=SMEM)] + [vmem] * (len(operands) - 1),
        out_specs=[vmem] * members if spread else vmem,
        scratch_shapes=[pltpu.VMEM((rows, dps * cols), F32)] if spread else [],
        compiler_params=params(),
        cost_estimate=cost(),
        name="output_projection",
    )(*operands)


def output_plain(place, hg, parts, weights, rows, group, order_h, order_t):
    dps, heads, hd, cols = weights[0].shape
    stacked = jnp.stack(weights).reshape(len(order_t), dps, len(order_h), group, hd, cols)
    stacked = jnp.take(stacked, place, axis=1)
    stacked = jnp.take(stacked, hg ^ jnp.array(order_h, jnp.int32), axis=2)
    total = None
    for j in range(group):
        left = jnp.concatenate([parts[2 * j], parts[2 * j + 1]], axis=0)
        left = left.transpose(2, 0, 1, 3).reshape(rows, -1)
        right = stacked[:, :, :, j].transpose(2, 0, 3, 1, 4).reshape(-1, dps * cols)
        term = dot(left, right)
        total = term if total is None else total + term
    return total.astype(BF16)


def collect_body(*refs):
    head = 0
    for piece in refs[:-1]:
        for j in range(piece.shape[1]):
            refs[-1][0, head, 0] = piece[0, j]
            head += 1


def collect_call(pieces):
    heads = sum(p.shape[1] for p in pieces)
    requests = pieces[0].shape[0]
    tail = pieces[0].shape[2:]
    return pl.pallas_call(
        collect_body,
        grid=(requests,),
        out_shape=jax.ShapeDtypeStruct((1, heads, requests) + tail, BF16),
        in_specs=[by_step(p) for p in pieces],
        out_specs=pl.BlockSpec((1, heads, 1) + tail, lambda r: (0, 0, r, 0, 0, 0)),
        compiler_params=params(),
        cost_estimate=cost(),
        name="collect_blocks",
    )(*pieces)


def residual_body(order_d, order_h, order_t, meta, hidden, *refs):
    pieces, out = refs[:-1], refs[-1]
    cols = pieces[0].shape[1] // len(order_d)
    nh, nt = len(order_h), len(order_t)
    for i, rel_h in enumerate(order_h):
        for t, rel_t in enumerate(order_t):
            piece = pieces[i * nt + t]
            for d, rel_d in enumerate(order_d):
                start = (((meta[0] ^ rel_d) * nh + (meta[2] ^ rel_h)) * nt + (meta[1] ^ rel_t)) * cols
                at = pl.ds(pl.multiple_of(start, cols), cols)
                summed = piece[:, d * cols : (d + 1) * cols].astype(F32)
                out[:, at] = (hidden[:, at].astype(F32) + summed).astype(BF16)


def residual_call(meta, hidden, pieces, order_d, order_h, order_t):
    vmem = pl.BlockSpec(memory_space=pltpu.VMEM)
    return pl.pallas_call(
        lambda *refs: residual_body(order_d, order_h, order_t, *refs),
        out_shape=jax.ShapeDtypeStruct(hidden.shape, BF16),
        in_specs=[pl.BlockSpec(memory_space=SMEM)] + [vmem] * (1 + len(pieces)),
        out_specs=vmem,
        compiler_params=params(),
        cost_estimate=cost(),
        name="residual",
    )(meta, hidden, *pieces)


def plane_swap(x, rel_h, rel_t):
    nt, nh = lax.axis_size("tp"), lax.axis_size("hg")
    pairs = [(t * nh + h, (t ^ rel_t) * nh + (h ^ rel_h)) for t in range(nt) for h in range(nh)]
    return lax.ppermute(x, ("tp", "hg"), pairs)


def head_gather(x, h_strides, t_strides, h_first, token=None):
    def over_h(x):
        for s in h_strides[:-1]:
            x = jnp.concatenate([x, swap(x, "hg", s)], axis=0)
        return x

    def over_t(x):
        for s in t_strides:
            x = jnp.concatenate([x, swap(x, "tp", s)], axis=1)
        return x

    first, second = (over_h, over_t) if h_first else (over_t, over_h)
    x = first(x[None, None])
    if token is not None:
        x = after(x, token)
    x = second(x)
    return [x, swap(x, "hg", h_strides[-1])]


def plan_of(group):
    if group % 4 == 0:
        q = group // 4
        return [2 * q, 2 * q], [(0, q, 2, 3), (q, q, 3, 4), (2 * q, 2 * q, 4, 4)]
    return [group], [(0, group, 3, 3)]


def on_device(hidden_in, norm_gain, qkv_weight, out_weight, cache_kv, cached_lengths, owner_table):
    nt, nh, nd = lax.axis_size("tp"), lax.axis_size("hg"), lax.axis_size("dp")
    tp, hg, dp = lax.axis_index("tp"), lax.axis_index("hg"), lax.axis_index("dp")
    local_rows, width = hidden_in.shape[2:]
    local_depth, _, local_heads, hd = qkv_weight.shape
    group = local_heads // nh
    depth = local_depth * nh
    rows = local_rows * nt * nh
    cap = (cache_kv.shape[2] + rows) // BLOCK // nd
    length = lax.dynamic_index_in_dim(cached_lengths, dp, 0, keepdims=False)

    far, all_d = halving(nd, 2), halving(nd, 1)
    own_rel = offsets(far)
    h_strides, t_strides = halving(nh, 1), halving(nt, 1)
    order_h, order_t = offsets(h_strides), offsets(t_strides)
    members = dp ^ jnp.arange(nd, dtype=jnp.int32)
    place = sum(jnp.where(members == rel, k, 0) for k, rel in enumerate(offsets(all_d))).astype(jnp.int32)
    meta = jnp.stack([dp, tp, hg, hg * group]).astype(jnp.int32)

    cols = out_weight.shape[2] // nt
    out_held = [out_weight]
    for s in far:
        out_held = out_held + hold([swap(w, "dp", s) for w in out_held], 60)
    by_head = qkv_weight.reshape(local_depth, 3, nh, group, hd).transpose(2, 3, 0, 1, 4)
    by_head = by_head.reshape(nh, group, local_depth, 3 * hd)
    sizes, finishing = plan_of(group)
    firsts = [sum(sizes[:c]) for c in range(len(sizes))]
    given = [by_head[:, f : f + size] for f, size in zip(firsts, sizes)]
    mine = [lax.all_to_all(given[0], "hg", 0, 0, tiled=True)]

    def over_h(x):
        for s in h_strides[:-1]:
            x = jnp.concatenate([x, swap(x, "hg", s)], axis=1)
        return x

    def over_t(x):
        for s in t_strides:
            x = jnp.concatenate([x, swap(x, "tp", s)], axis=2)
        return x

    own, sent = norm_call(meta, after(hidden_in[0, 0], given[0]), norm_gain.reshape(1, width), depth, own_rel)
    cut = len(own_rel) // 2
    own, pair = own[:, None, None], swap(sent, "dp", 1)[:, None, None]
    own = [over_t(over_h(own[:cut])), over_h(over_t(own[cut:]))]
    pair = [pair[:cut], pair[cut:]]

    positions = length + jnp.arange(rows, dtype=jnp.int32)
    half_rot = ROT // 2
    frequency = 10000.0 ** (-2.0 * jnp.arange(half_rot, dtype=F32) / ROT)
    angles = positions.astype(F32)[:, None] * frequency[None, :]
    cos_half, sin_half = jnp.cos(angles), jnp.sin(angles)
    cosine = jnp.concatenate([cos_half, cos_half, jnp.ones((rows, hd - ROT), F32)], axis=1)
    sine = jnp.concatenate([-sin_half, sin_half, jnp.zeros((rows, hd - ROT), F32)], axis=1)
    live = dict(out=out_held, mine=mine, given=given[1:], own=own, pair=pair)
    live["tables"] = (cosine, sine)
    live = lax.optimization_barrier(live)

    weights, arrived, ready, placed = [], {}, {}, {}
    handed, gathered = {}, {}
    chunks = len(sizes)
    places = [(c, i) for c, size in enumerate(sizes) for i in range(size)]
    last_stage = chunks + 2
    for stage in range(1, last_stage + 1):
        if stage <= chunks:
            held = [live["mine"][stage - 1]]
            for s in far:
                held = held + hold([swap(w, "dp", s) for w in held], 60)
            weights.append(held)
        if stage == 1:
            live["mine"] = live["mine"] + [lax.all_to_all(g, "hg", 0, 0, tiled=True) for g in live.pop("given")]
            pair = [over_t(over_h(live["pair"][0])), over_h(over_t(live["pair"][1]))]
            live["pair"] = pair + [swap(x, "hg", h_strides[-1]) for x in pair]
            live["out"] = live["out"] + hold([swap(w, "dp", 1) for w in live["out"]], 45)
            own = after(live["own"], tuple(live["pair"]))
            live["own"] = own + [swap(x, "hg", h_strides[-1]) for x in own]
        for first, _, at, handover in finishing:
            if at < handover == stage:
                handed[first] = lax.all_to_all(live["placed"][first], "dp", 0, 0, tiled=True)
                if stage < last_stage:
                    (handed[first],) = hold([handed[first]], 40)
        for first, count, at, _ in finishing:
            c, i = places[first]
            if c + 2 == stage:
                partial = partner_call(live["pair"], live["weights"][c], rows, i, count)
                arrived[first] = swap(partial, "dp", 1)
                if c + 1 == chunks:
                    (arrived[first],) = hold([arrived[first]], 40)
        if stage == 2:
            held = split_call(meta, after(live["out"], partial), order_t)
            live["out"] = [swap(w, "tp", r) if r else w for w, r in zip(held, order_t)]
        for first, count, at, _ in finishing:
            if at == stage - 1 and first not in gathered:
                gathered[first] = [
                    head_gather(live["ready"][first][i], h_strides, t_strides, i % 2 == 0, partial)
                    for i in range(count)
                ]
        for first, count, at, handover in finishing:
            if at == stage:
                c, i = places[first]
                query, kv, placed[first] = finish_call(
                    meta, cached_lengths, owner_table, live["own"], live["weights"][c], arrived[first],
                    *live["tables"], cache_kv, i, first, cap, nd, (order_h, order_t),
                )
                ready[first] = attend_call(meta, cached_lengths, query, kv, cache_kv, first)
                if 2 < at < last_stage:
                    gathered[first] = [
                        head_gather(ready[first][n], h_strides, t_strides, n % 2 == 1) for n in range(count)
                    ]
                if at == handover:
                    blocks = after(placed[first], ready[first])
                    handed[first] = lax.all_to_all(blocks, "dp", 0, 0, tiled=True)
        if stage == last_stage:
            break
        live.update(weights=weights, arrived=arrived, ready=ready, placed=placed, handed=handed, gathered=gathered)
        live = lax.optimization_barrier(live)
        weights = list(live["weights"])
        arrived, ready, placed = dict(live["arrived"]), dict(live["ready"]), dict(live["placed"])
        handed, gathered = dict(live["handed"]), dict(live["gathered"])

    out_weights = live["out"]
    first, count, _, _ = finishing[-1]
    done = sorted(gathered)
    summed = None
    if done and cols % 128 == 0:
        parts = [p for f in done for head in gathered[f] for p in head]
        summed = output_call(meta, parts, out_weights, rows, 0, group, order_h, order_t)
    gathered[first] = [
        head_gather(ready[first][i], h_strides, t_strides, i % 2 == 0, summed) for i in range(count)
    ]
    if cols % 128 == 0:
        parts = [p for head in gathered[first] for p in head]
        pieces = output_call(meta, parts, out_weights, rows, first, group, order_h, order_t, summed, True)
        rels = [(h, t) for h in order_h for t in order_t]
        pieces = [plane_swap(p, h, t) if h or t else p for p, (h, t) in zip(pieces, rels)]
        hidden_out = residual_call(meta, hidden_in[0, 0], pieces, offsets(all_d), order_h, order_t)
    else:
        parts = [p for f in sorted(gathered) for head in gathered[f] for p in head]
        summed = output_plain(place, hg, parts, out_weights, rows, group, order_h, order_t)
        summed = lax.all_to_all(
            summed.reshape(nh * nt, local_rows, nd * cols), ("hg", "tp"), 0, 0, tiled=True
        )
        summed = summed.reshape(nh, nt, local_rows, nd, cols).transpose(2, 3, 0, 1, 4).reshape(local_rows, width)
        hidden_out = (hidden_in[0, 0].astype(F32) + summed.astype(F32)).astype(BF16)
    handed = [handed[f] for f, _, _, _ in finishing]
    return hidden_out[None, None], collect_call(handed)


def solution(mesh):
    return jax.shard_map(
        on_device,
        mesh=mesh,
        in_specs=(
            P("dp", "hg", "tp", None),
            P(),
            P(("dp", "hg"), None, "tp", None),
            P("tp", None, ("dp", "hg")),
            P("dp", "tp", None, None),
            P(),
            P(),
        ),
        out_specs=(P("dp", "hg", "tp", None), P("dp", ("tp", "hg"), None, None, None, None)),
        check_vma=False,
    )
```

```python
import math

import jax
import jax.numpy as jnp
from jax import lax
from jax.experimental import pallas as pl
from jax.experimental.pallas import tpu as pltpu
from jax.sharding import PartitionSpec as P

ROT = 32
BLOCK = 128
EPSILON = 1e-05
VMEM_LIMIT = 48 * 1024 * 1024

SMEM = pltpu.SMEM
BF16 = jnp.bfloat16
F32 = jnp.float32


def params():
    return pltpu.CompilerParams(vmem_limit_bytes=VMEM_LIMIT)


def cost():
    return pl.CostEstimate(flops=1, bytes_accessed=1, transcendentals=0)


def hold(xs, microseconds):
    hbm = pl.BlockSpec(memory_space=pl.ANY)
    held = pl.pallas_call(
        lambda *refs: None,
        out_shape=[jax.ShapeDtypeStruct(x.shape, x.dtype) for x in xs],
        in_specs=[hbm] * len(xs),
        out_specs=[hbm] * len(xs),
        input_output_aliases={i: i for i in range(len(xs))},
        cost_estimate=pl.CostEstimate(flops=int(microseconds * 1e9), bytes_accessed=1, transcendentals=0),
        name="hold",
    )(*xs)
    return list(held)


def swap(x, axis, stride):
    size = lax.axis_size(axis)
    return lax.ppermute(x, axis, [(i, i ^ stride) for i in range(size)])


def halving(size, last):
    strides = []
    step = size // 2
    while step >= last:
        strides.append(step)
        step //= 2
    return strides


def offsets(strides):
    order = [0]
    for stride in strides:
        order = order + [o ^ stride for o in order]
    return order


def after(value, token):
    return lax.optimization_barrier((value, token))[0]


def dot(a, b):
    return jnp.dot(a, b, preferred_element_type=F32)


def dot_t(a, b):
    return lax.dot_general(a, b, (((1,), (1,)), ((), ())), preferred_element_type=F32)


def norm_body(depth, own_rel, meta, hidden, gain, own, sent, scratch):
    rows = hidden[...].astype(F32)
    centered = rows - jnp.mean(rows, axis=-1, keepdims=True)
    spread = jnp.mean(centered * centered, axis=-1, keepdims=True)
    scratch[...] = (centered * lax.rsqrt(spread + EPSILON) * gain[...]).astype(BF16)
    me = meta[0]
    for e, rel in enumerate(own_rel):
        start = pl.multiple_of((me ^ rel) * depth, 128)
        own[e] = scratch[:, pl.ds(start, depth)]
        start = pl.multiple_of((me ^ rel ^ 1) * depth, 128)
        sent[e] = scratch[:, pl.ds(start, depth)]


def norm_call(meta, hidden, gain, depth, own_rel):
    rows, width = hidden.shape
    shape = jax.ShapeDtypeStruct((len(own_rel), rows, depth), BF16)
    return pl.pallas_call(
        lambda *refs: norm_body(depth, own_rel, *refs),
        out_shape=(shape, shape),
        in_specs=[
            pl.BlockSpec(memory_space=SMEM),
            pl.BlockSpec(memory_space=pltpu.VMEM),
            pl.BlockSpec(memory_space=pltpu.VMEM),
        ],
        out_specs=(pl.BlockSpec(memory_space=pltpu.VMEM), pl.BlockSpec(memory_space=pltpu.VMEM)),
        scratch_shapes=[pltpu.VMEM((rows, width), BF16)],
        compiler_params=params(),
        cost_estimate=cost(),
        name="layer_norm",
    )(meta, hidden, gain)


def load_weights(refs):
    return [ref[:, 0].reshape(-1, ref.shape[-1]) for ref in refs]


def product(xs, ws, total):
    half = total.shape[0] // 2
    streams = len(xs) // 2
    for core in (0, 1):
        result = None
        k = 0
        for x in xs[core * streams : (core + 1) * streams]:
            for e in range(x.shape[0]):
                term = dot(x[e].reshape(-1, x.shape[-1]), ws[k])
                result = term if result is None else result + term
                k += 1
        total[core * half : (core + 1) * half] = result.astype(total.dtype)


def whole(x):
    nd = len(x.shape)
    return pl.BlockSpec(x.shape, lambda *_: (0,) * nd)


def by_step(x, first=0):
    nd = len(x.shape) - 1
    return pl.BlockSpec((1,) + tuple(x.shape[1:]), lambda i, *_: (first + i,) + (0,) * nd)


def weight_specs(ws, first):
    return [pl.BlockSpec((w.shape[0], 1) + w.shape[2:], lambda i, *_: (0, first + i, 0, 0)) for w in ws]


def partner_body(inputs, *refs):
    product(refs[:inputs], load_weights(refs[inputs:-1]), refs[-1].at[0])


def partner_call(xs, ws, rows, at, heads=1):
    out = jax.ShapeDtypeStruct((heads, rows, ws[0].shape[-1]), BF16)
    return pl.pallas_call(
        lambda *refs: partner_body(len(xs), *refs),
        grid=(heads,),
        out_shape=out,
        in_specs=[whole(x) for x in xs] + weight_specs(ws, at),
        out_specs=by_step(out),
        compiler_params=params(),
        cost_estimate=cost(),
        name="partner_product",
    )(*xs, *ws)


def finish_body(inputs, cap, order_h, order_t, meta, lengths, owners, *refs):
    xs, ws = refs[:inputs], load_weights(refs[inputs:-10])
    arrived, cosine, sine, cache, query, kv, placed, total, slots, counts = refs[-10:]
    me, tp, hg = meta[0], meta[1], meta[2]
    product(xs, ws, total)
    hd = query.shape[2]
    members = [(h, t) for h in order_h for t in order_t]
    run_rows = total.shape[0] // len(members)
    lane = lax.broadcasted_iota(jnp.int32, (run_rows, hd), 1)
    half_rot = ROT // 2
    for m, (rel_h, rel_t) in enumerate(members):
        rows = slice(m * run_rows, (m + 1) * run_rows)
        start = pl.multiple_of(((hg ^ rel_h) * len(order_t) + (tp ^ rel_t)) * run_rows, run_rows)
        to = pl.ds(start, run_rows)
        cos_rows, sin_rows = cosine[to], sine[to]

        def summed(low):
            return total[rows, low : low + hd] + arrived[0, rows, low : low + hd].astype(F32)

        def rotated(part):
            other = jnp.where(
                lane < half_rot, pltpu.roll(part, hd - half_rot, 1), pltpu.roll(part, half_rot, 1)
            )
            return (part * cos_rows + other * sin_rows).astype(BF16)

        query[0, to] = rotated(summed(0))
        kv[0, to, :hd] = rotated(summed(hd))
        kv[0, to, hd:] = summed(2 * hd).astype(BF16)
    owner_count = placed.shape[0]
    blocks = owners.shape[1]
    cached_blocks = lengths[me] // BLOCK
    valid_end = cached_blocks + query.shape[1] // BLOCK
    for s in range(owner_count * cap):
        slots[s] = -1
    for o in range(owner_count):
        counts[o] = 0
    for b in range(blocks):

        @pl.when(b < valid_end)
        def _():
            owner = owners[me, b]
            rank = counts[owner]

            @pl.when(rank < cap)
            def _():
                slots[owner * cap + rank] = b

            counts[owner] = rank + 1

    for s in range(owner_count * cap):
        block = slots[s]
        o, c = divmod(s, cap)

        @pl.when(block < 0)
        def _():
            placed[o, 0, c] = jnp.zeros(placed.shape[3:], BF16)

        @pl.when((block >= 0) & (block < cached_blocks))
        def _():
            at = pl.multiple_of(block * BLOCK, BLOCK)
            placed[o, 0, c] = cache[0, 0, pl.ds(at, BLOCK)]

        @pl.when(block >= cached_blocks)
        def _():
            at = pl.multiple_of((block - cached_blocks) * BLOCK, BLOCK)
            placed[o, 0, c] = kv[0, pl.ds(at, BLOCK)]


def cache_by_step(cache, first):
    return pl.BlockSpec((1, 1) + cache.shape[2:], lambda i, meta, *_: (0, meta[3] + first + i, 0, 0))


def finish_call(meta, lengths, owners, xs, ws, arrived, cosine, sine, cache, at, first, cap, owner_count, orders):
    heads, rows, width = arrived.shape
    hd = width // 3
    cache_spec = cache_by_step(cache, first)
    outs = [(heads, rows, hd), (heads, rows, 2 * hd), (owner_count, heads, cap, BLOCK, 2 * hd)]
    outs = tuple(jax.ShapeDtypeStruct(o, BF16) for o in outs)
    placed_spec = pl.BlockSpec((owner_count, 1, cap, BLOCK, 2 * hd), lambda i, *_: (0, i, 0, 0, 0))
    return pl.pallas_call(
        lambda *refs: finish_body(len(xs), cap, *orders, *refs),
        out_shape=outs,
        grid_spec=pltpu.PrefetchScalarGridSpec(
            num_scalar_prefetch=3,
            grid=(heads,),
            in_specs=[whole(x) for x in xs]
            + weight_specs(ws, at)
            + [by_step(arrived), whole(cosine), whole(sine), cache_spec],
            out_specs=(by_step(outs[0]), by_step(outs[1]), placed_spec),
            scratch_shapes=[
                pltpu.VMEM((rows, width), F32),
                pltpu.SMEM((owner_count * cap,), jnp.int32),
                pltpu.SMEM((owner_count,), jnp.int32),
            ],
        ),
        compiler_params=params(),
        cost_estimate=cost(),
        name="finish_projection",
    )(meta, lengths, owners, *xs, *ws, arrived, cosine, sine, cache)


def attend_body(q_rows, meta, lengths, query, kv, cache, out):
    hd = query.shape[2]
    length = lengths[meta[0]]
    factor = math.log2(math.e) / math.sqrt(hd)
    old_col = lax.broadcasted_iota(jnp.int32, (q_rows, cache.shape[2]), 1)
    causal = lax.broadcasted_iota(jnp.int32, (q_rows, q_rows), 1) <= lax.broadcasted_iota(
        jnp.int32, (q_rows, q_rows), 0
    )
    for step in range(query.shape[1] // q_rows):
        first = step * q_rows
        q = query[0, first : first + q_rows]
        old = jnp.where(old_col < length, dot_t(q, cache[0, 0, :, :hd]), -jnp.inf)
        diag = jnp.where(causal, dot_t(q, kv[0, first : first + q_rows, :hd]), -jnp.inf)
        top = jnp.maximum(jnp.max(old, axis=1, keepdims=True), jnp.max(diag, axis=1, keepdims=True))
        if step:
            new = dot_t(q, kv[0, :first, :hd])
            top = jnp.maximum(top, jnp.max(new, axis=1, keepdims=True))
        old = jnp.exp2((old - top) * factor)
        diag = jnp.exp2((diag - top) * factor)
        total = jnp.sum(old, axis=1, keepdims=True) + jnp.sum(diag, axis=1, keepdims=True)
        result = dot(old.astype(BF16), cache[0, 0, :, hd:]) + dot(diag.astype(BF16), kv[0, first : first + q_rows, hd:])
        if step:
            new = jnp.exp2((new - top) * factor)
            total = total + jnp.sum(new, axis=1, keepdims=True)
            result = result + dot(new.astype(BF16), kv[0, :first, hd:])
        out[0, first : first + q_rows] = (result / total).astype(BF16)


def attend_call(meta, lengths, query, kv, cache, first, q_rows=256):
    heads, rows, hd = query.shape
    out = jax.ShapeDtypeStruct((heads, rows, hd), BF16)
    return pl.pallas_call(
        lambda *refs: attend_body(q_rows, *refs),
        out_shape=out,
        grid_spec=pltpu.PrefetchScalarGridSpec(
            num_scalar_prefetch=2,
            grid=(heads,),
            in_specs=[by_step(query), by_step(kv), cache_by_step(cache, first)],
            out_specs=by_step(out),
        ),
        compiler_params=params(),
        cost_estimate=cost(),
        name="attention",
    )(meta, lengths, query, kv, cache)


def split_body(order_t, meta, *refs):
    held, outs = refs[: -len(order_t)], refs[-len(order_t) :]
    cols = outs[0].shape[-1]
    for r, out in zip(order_t, outs):
        start = pl.multiple_of((meta[1] ^ r) * cols, cols)
        for d, ref in enumerate(held):
            out[d] = ref[:, :, pl.ds(start, cols)]


def split_call(meta, held, order_t):
    heads, hd, width = held[0].shape
    cols = width // len(order_t)
    if cols % 128:
        stacked = jnp.stack(held).reshape(len(held), heads, hd, len(order_t), cols)
        return [lax.dynamic_index_in_dim(stacked, meta[1] ^ r, 3, keepdims=False) for r in order_t]
    vmem = pl.BlockSpec(memory_space=pltpu.VMEM)
    return pl.pallas_call(
        lambda *refs: split_body(order_t, *refs),
        out_shape=[jax.ShapeDtypeStruct((len(held), heads, hd, cols), BF16) for _ in order_t],
        in_specs=[pl.BlockSpec(memory_space=SMEM)] + [vmem] * len(held),
        out_specs=[vmem] * len(order_t),
        compiler_params=params(),
        cost_estimate=cost(),
        name="split_columns",
    )(meta, *held)


def output_body(first, heads, group, order_h, order_t, with_sum, spread, meta, *refs):
    pieces = len(order_h) * len(order_t)
    parts, weights = refs[: 2 * heads], refs[2 * heads : 2 * heads + len(order_t)]
    rest = refs[2 * heads + len(order_t) :]
    tp, hg = meta[1], meta[2]
    total = rest[0][...] if with_sum else None
    for j in range(heads):
        left, right = [], []
        for i, rel_h in enumerate(order_h):
            core, h = divmod(i, len(order_h) // 2)
            for t in range(len(order_t)):
                left.append(parts[2 * j + core][h, t])
                head = (hg ^ rel_h) * group + first + j
                right.append(jnp.concatenate([weights[t][d, head] for d in range(weights[t].shape[0])], axis=1))
        term = dot(jnp.concatenate(left, axis=1), jnp.concatenate(right, axis=0))
        total = term if total is None else total + term
    if not spread:
        rest[-1][...] = total
        return
    scratch, outs = rest[-1], rest[-1 - pieces : -1]
    scratch[...] = total
    run_rows = outs[0].shape[0]
    for i, rel_h in enumerate(order_h):
        for t, rel_t in enumerate(order_t):
            start = pl.multiple_of(((hg ^ rel_h) * len(order_t) + (tp ^ rel_t)) * run_rows, run_rows)
            outs[i * len(order_t) + t][...] = scratch[pl.ds(start, run_rows)].astype(BF16)


def output_call(meta, parts, weights, rows, first, group, order_h, order_t, total=None, spread=False):
    members = len(order_h) * len(order_t)
    dps, cols = weights[0].shape[0], weights[0].shape[-1]
    vmem = pl.BlockSpec(memory_space=pltpu.VMEM)
    operands = (meta, *parts, *weights) + (() if total is None else (total,))
    heads = len(parts) // 2
    out = jax.ShapeDtypeStruct((rows, dps * cols), F32)
    piece = jax.ShapeDtypeStruct((rows // members, dps * cols), BF16)
    return pl.pallas_call(
        lambda *refs: output_body(first, heads, group, order_h, order_t, total is not None, spread, *refs),
        out_shape=[piece] * members if spread else out,
        in_specs=[pl.BlockSpec(memory_space=SMEM)] + [vmem] * (len(operands) - 1),
        out_specs=[vmem] * members if spread else vmem,
        scratch_shapes=[pltpu.VMEM((rows, dps * cols), F32)] if spread else [],
        compiler_params=params(),
        cost_estimate=cost(),
        name="output_projection",
    )(*operands)


def output_plain(place, hg, parts, weights, rows, group, order_h, order_t):
    dps, heads, hd, cols = weights[0].shape
    stacked = jnp.stack(weights).reshape(len(order_t), dps, len(order_h), group, hd, cols)
    stacked = jnp.take(stacked, place, axis=1)
    stacked = jnp.take(stacked, hg ^ jnp.array(order_h, jnp.int32), axis=2)
    total = None
    for j in range(group):
        left = jnp.concatenate([parts[2 * j], parts[2 * j + 1]], axis=0)
        left = left.transpose(2, 0, 1, 3).reshape(rows, -1)
        right = stacked[:, :, :, j].transpose(2, 0, 3, 1, 4).reshape(-1, dps * cols)
        term = dot(left, right)
        total = term if total is None else total + term
    return total.astype(BF16)


def collect_body(count, *refs):
    head = 0
    for piece in refs[:count]:
        for j in range(piece.shape[1]):
            refs[-1][0, head, 0] = piece[0, j]
            head += 1


def collect_call(pieces, heads, first, base=None):
    count = sum(p.shape[1] for p in pieces)
    requests = pieces[0].shape[0]
    tail = pieces[0].shape[2:]
    based = [] if base is None else [base]
    return pl.pallas_call(
        lambda *refs: collect_body(len(pieces), *refs),
        grid=(requests,),
        out_shape=jax.ShapeDtypeStruct((1, heads, requests) + tail, BF16),
        in_specs=[by_step(p) for p in pieces] + [pl.BlockSpec(memory_space=pl.ANY)] * len(based),
        out_specs=pl.BlockSpec((1, count, 1) + tail, lambda r: (0, first // count, r, 0, 0, 0)),
        input_output_aliases={len(pieces): 0} if based else {},
        compiler_params=params(),
        cost_estimate=cost(),
        name="collect_blocks",
    )(*pieces, *based)


def residual_body(order_d, order_h, order_t, meta, hidden, *refs):
    pieces, out = refs[:-1], refs[-1]
    cols = pieces[0].shape[1] // len(order_d)
    nh, nt = len(order_h), len(order_t)
    for i, rel_h in enumerate(order_h):
        for t, rel_t in enumerate(order_t):
            piece = pieces[i * nt + t]
            for d, rel_d in enumerate(order_d):
                start = (((meta[0] ^ rel_d) * nh + (meta[2] ^ rel_h)) * nt + (meta[1] ^ rel_t)) * cols
                at = pl.ds(pl.multiple_of(start, cols), cols)
                summed = piece[:, d * cols : (d + 1) * cols].astype(F32)
                out[:, at] = (hidden[:, at].astype(F32) + summed).astype(BF16)


def residual_call(meta, hidden, pieces, order_d, order_h, order_t):
    vmem = pl.BlockSpec(memory_space=pltpu.VMEM)
    return pl.pallas_call(
        lambda *refs: residual_body(order_d, order_h, order_t, *refs),
        out_shape=jax.ShapeDtypeStruct(hidden.shape, BF16),
        in_specs=[pl.BlockSpec(memory_space=SMEM)] + [vmem] * (1 + len(pieces)),
        out_specs=vmem,
        compiler_params=params(),
        cost_estimate=cost(),
        name="residual",
    )(meta, hidden, *pieces)


def plane_swap(x, rel_h, rel_t):
    nt, nh = lax.axis_size("tp"), lax.axis_size("hg")
    pairs = [(t * nh + h, (t ^ rel_t) * nh + (h ^ rel_h)) for t in range(nt) for h in range(nh)]
    return lax.ppermute(x, ("tp", "hg"), pairs)


def head_gather(x, h_strides, t_strides, h_first, token=None):
    def over_h(x):
        for s in h_strides[:-1]:
            x = jnp.concatenate([x, swap(x, "hg", s)], axis=0)
        return x

    def over_t(x):
        for s in t_strides:
            x = jnp.concatenate([x, swap(x, "tp", s)], axis=1)
        return x

    first, second = (over_h, over_t) if h_first else (over_t, over_h)
    x = first(x[None, None])
    if token is not None:
        x = after(x, token)
    x = second(x)
    return [x, swap(x, "hg", h_strides[-1])]


def plan_of(group):
    if group % 4 == 0:
        q = group // 4
        return [2 * q, 2 * q], [(0, q, 2, 3), (q, q, 3, 4), (2 * q, 2 * q, 4, 4)]
    return [group], [(0, group, 3, 3)]


def on_device(hidden_in, norm_gain, qkv_weight, out_weight, cache_kv, cached_lengths, owner_table):
    nt, nh, nd = lax.axis_size("tp"), lax.axis_size("hg"), lax.axis_size("dp")
    tp, hg, dp = lax.axis_index("tp"), lax.axis_index("hg"), lax.axis_index("dp")
    local_rows, width = hidden_in.shape[2:]
    local_depth, _, local_heads, hd = qkv_weight.shape
    group = local_heads // nh
    depth = local_depth * nh
    rows = local_rows * nt * nh
    cap = (cache_kv.shape[2] + rows) // BLOCK // nd
    length = lax.dynamic_index_in_dim(cached_lengths, dp, 0, keepdims=False)

    far, all_d = halving(nd, 2), halving(nd, 1)
    own_rel = offsets(far)
    h_strides, t_strides = halving(nh, 1), halving(nt, 1)
    order_h, order_t = offsets(h_strides), offsets(t_strides)
    members = dp ^ jnp.arange(nd, dtype=jnp.int32)
    place = sum(jnp.where(members == rel, k, 0) for k, rel in enumerate(offsets(all_d))).astype(jnp.int32)
    meta = jnp.stack([dp, tp, hg, hg * group]).astype(jnp.int32)

    cols = out_weight.shape[2] // nt
    out_held = [out_weight]
    for s in far[:-1]:
        out_held = out_held + [swap(w, "dp", s) for w in out_held]
    *come, out_near = hold([swap(w, "dp", far[-1]) for w in out_held] + [swap(out_weight, "dp", 1)], 60)
    out_held = out_held + come
    by_head = qkv_weight.reshape(local_depth, 3, nh, group, hd).transpose(2, 3, 0, 1, 4)
    by_head = by_head.reshape(nh, group, local_depth, 3 * hd)
    sizes, finishing = plan_of(group)
    firsts = [sum(sizes[:c]) for c in range(len(sizes))]
    given = [by_head[:, f : f + size] for f, size in zip(firsts, sizes)]
    mine = [lax.all_to_all(given[0], "hg", 0, 0, tiled=True)]

    def over_h(x):
        for s in h_strides[:-1]:
            x = jnp.concatenate([x, swap(x, "hg", s)], axis=1)
        return x

    def over_t(x):
        for s in t_strides:
            x = jnp.concatenate([x, swap(x, "tp", s)], axis=2)
        return x

    own, sent = norm_call(meta, after(hidden_in[0, 0], given[0]), norm_gain.reshape(1, width), depth, own_rel)
    cut = len(own_rel) // 2
    own, pair = own[:, None, None], swap(sent, "dp", 1)[:, None, None]
    own = [over_t(over_h(own[:cut])), over_h(over_t(own[cut:]))]
    pair = [pair[:cut], pair[cut:]]

    positions = length + jnp.arange(rows, dtype=jnp.int32)
    half_rot = ROT // 2
    frequency = 10000.0 ** (-2.0 * jnp.arange(half_rot, dtype=F32) / ROT)
    angles = positions.astype(F32)[:, None] * frequency[None, :]
    cos_half, sin_half = jnp.cos(angles), jnp.sin(angles)
    cosine = jnp.concatenate([cos_half, cos_half, jnp.ones((rows, hd - ROT), F32)], axis=1)
    sine = jnp.concatenate([-sin_half, sin_half, jnp.zeros((rows, hd - ROT), F32)], axis=1)
    live = dict(out=out_held, near=out_near, mine=mine, given=given[1:], own=own, pair=pair)
    live["tables"] = (cosine, sine)
    live = lax.optimization_barrier(live)

    weights, arrived, ready, placed = [], {}, {}, {}
    handed, gathered = {}, {}
    chunks = len(sizes)
    places = [(c, i) for c, size in enumerate(sizes) for i in range(size)]
    last_stage = chunks + 2
    for stage in range(1, last_stage + 1):
        if stage <= chunks:
            held = [live["mine"][stage - 1]]
            for s in far[:-1]:
                held = held + [swap(w, "dp", s) for w in held]
            come = [swap(w, "dp", far[-1]) for w in held]
            with_out = [swap(w, "dp", 1) for w in live["out"][1:]] if stage == 1 else []
            come = hold(come + with_out, 150)
            weights.append(held + come[: len(held)])
            if stage == 1:
                live["out"] = live["out"] + [live.pop("near")] + come[len(held) :]
        if stage == 1:
            live["mine"] = live["mine"] + [lax.all_to_all(g, "hg", 0, 0, tiled=True) for g in live.pop("given")]
            pair = [over_t(over_h(live["pair"][0])), over_h(over_t(live["pair"][1]))]
            live["pair"] = pair + [swap(x, "hg", h_strides[-1]) for x in pair]
            own = after(live["own"], tuple(live["pair"]))
            live["own"] = own + [swap(x, "hg", h_strides[-1]) for x in own]
        moved = [f for f, _, at, handover in finishing if at < handover == stage]
        come = [lax.all_to_all(live["placed"][f], "dp", 0, 0, tiled=True) for f in moved]
        sent = []
        for first, count, at, _ in finishing:
            c, i = places[first]
            if c + 2 == stage:
                partial = partner_call(live["pair"], live["weights"][c], rows, i, count)
                arrived[first] = swap(partial, "dp", 1)
                sent.append(first)
        if stage == chunks + 1:
            come = hold(come + [arrived[f] for f in sent], 60)
            arrived.update(zip(sent, come[len(moved) :]))
        handed.update(zip(moved, come))
        if stage == 2:
            held = split_call(meta, after(live["out"], partial), order_t)
            live["out"] = [swap(w, "tp", r) if r else w for w, r in zip(held, order_t)]
        for first, count, at, _ in finishing:
            if at == stage - 1 and first not in gathered:
                gathered[first] = [
                    head_gather(after(live["ready"][first], partial)[i], h_strides, t_strides, i % 2 == 0)
                    for i in range(count)
                ]
        for first, count, at, handover in finishing:
            if at == stage:
                c, i = places[first]
                come = live["arrived"].get(first)
                come = arrived[first] if come is None else come
                if 2 < at < last_stage:
                    come = after(come, partial)
                query, kv, placed[first] = finish_call(
                    meta, cached_lengths, owner_table, live["own"], live["weights"][c], come,
                    *live["tables"], cache_kv, i, first, cap, nd, (order_h, order_t),
                )
                ready[first] = attend_call(meta, cached_lengths, query, kv, cache_kv, first)
                if 2 < at < last_stage:
                    gathered[first] = [
                        head_gather(ready[first][n], h_strides, t_strides, n % 2 == 1) for n in range(count)
                    ]
                if at == handover:
                    blocks = after(placed[first], ready[first])
                    handed[first] = lax.all_to_all(blocks, "dp", 0, 0, tiled=True)
        if stage == last_stage:
            break
        live.update(weights=weights, arrived=arrived, ready=ready, placed=placed, handed=handed, gathered=gathered)
        live = lax.optimization_barrier(live)
        weights = list(live["weights"])
        arrived, ready, placed = dict(live["arrived"]), dict(live["ready"]), dict(live["placed"])
        handed, gathered = dict(live["handed"]), dict(live["gathered"])

    out_weights = live["out"]
    first, count, _, _ = finishing[-1]
    done = sorted(gathered)
    summed = None
    if done and cols % 128 == 0:
        parts = [p for f in done for head in gathered[f] for p in head]
        summed = output_call(meta, parts, out_weights, rows, 0, group, order_h, order_t)
    gathered[first] = [
        head_gather(ready[first][i], h_strides, t_strides, i % 2 == 0, summed) for i in range(count)
    ]
    collected = None
    if cols % 128 == 0:
        parts = [p for head in gathered[first] for p in head]
        pieces = output_call(meta, parts, out_weights, rows, first, group, order_h, order_t, summed, True)
        rels = [(h, t) for h in order_h for t in order_t]
        pieces = [plane_swap(p, h, t) if h or t else p for p, (h, t) in zip(pieces, rels)]
        if 2 * count == group:
            early = [handed[f] for f, _, _, _ in finishing[:-1]]
            collected = collect_call(early, group, 0)
            pieces[0] = after(pieces[0], collected)
        hidden_out = residual_call(meta, hidden_in[0, 0], pieces, offsets(all_d), order_h, order_t)
    else:
        parts = [p for f in sorted(gathered) for head in gathered[f] for p in head]
        summed = output_plain(place, hg, parts, out_weights, rows, group, order_h, order_t)
        summed = lax.all_to_all(
            summed.reshape(nh * nt, local_rows, nd * cols), ("hg", "tp"), 0, 0, tiled=True
        )
        summed = summed.reshape(nh, nt, local_rows, nd, cols).transpose(2, 3, 0, 1, 4).reshape(local_rows, width)
        hidden_out = (hidden_in[0, 0].astype(F32) + summed.astype(F32)).astype(BF16)
    if collected is not None:
        collected = collect_call([handed[first]], group, first, collected)
    else:
        collected = collect_call([handed[f] for f, _, _, _ in finishing], group, 0)
    return hidden_out[None, None], collected


def solution(mesh):
    return jax.shard_map(
        on_device,
        mesh=mesh,
        in_specs=(
            P("dp", "hg", "tp", None),
            P(),
            P(("dp", "hg"), None, "tp", None),
            P("tp", None, ("dp", "hg")),
            P("dp", "tp", None, None),
            P(),
            P(),
        ),
        out_specs=(P("dp", "hg", "tp", None), P("dp", ("tp", "hg"), None, None, None, None)),
        check_vma=False,
    )
```

```python
import math

import jax
import jax.numpy as jnp
from jax import lax
from jax.experimental import pallas as pl
from jax.experimental.pallas import tpu as pltpu
from jax.sharding import PartitionSpec as P

ROT = 32
BLOCK = 128
EPSILON = 1e-05
VMEM_LIMIT = 48 * 1024 * 1024

SMEM = pltpu.SMEM
BF16 = jnp.bfloat16
F32 = jnp.float32


def params():
    return pltpu.CompilerParams(vmem_limit_bytes=VMEM_LIMIT)


def cost(microseconds=0):
    return pl.CostEstimate(flops=1 + int(microseconds * 1e9), bytes_accessed=1, transcendentals=0)


def hold(xs, microseconds):
    hbm = pl.BlockSpec(memory_space=pl.ANY)
    held = pl.pallas_call(
        lambda *refs: None,
        out_shape=[jax.ShapeDtypeStruct(x.shape, x.dtype) for x in xs],
        in_specs=[hbm] * len(xs),
        out_specs=[hbm] * len(xs),
        input_output_aliases={i: i for i in range(len(xs))},
        cost_estimate=pl.CostEstimate(flops=int(microseconds * 1e9), bytes_accessed=1, transcendentals=0),
        name="hold",
    )(*xs)
    return list(held)


def swap(x, axis, stride):
    size = lax.axis_size(axis)
    return lax.ppermute(x, axis, [(i, i ^ stride) for i in range(size)])


def halving(size, last):
    strides = []
    step = size // 2
    while step >= last:
        strides.append(step)
        step //= 2
    return strides


def offsets(strides):
    order = [0]
    for stride in strides:
        order = order + [o ^ stride for o in order]
    return order


def after(value, token):
    return lax.optimization_barrier((value, token))[0]


def dot(a, b):
    return jnp.dot(a, b, preferred_element_type=F32)


def dot_t(a, b):
    return lax.dot_general(a, b, (((1,), (1,)), ((), ())), preferred_element_type=F32)


def norm_body(depth, own_rel, meta, hidden, gain, own, sent, scratch):
    rows = hidden[...].astype(F32)
    centered = rows - jnp.mean(rows, axis=-1, keepdims=True)
    spread = jnp.mean(centered * centered, axis=-1, keepdims=True)
    scratch[...] = (centered * lax.rsqrt(spread + EPSILON) * gain[...]).astype(BF16)
    me = meta[0]
    for e, rel in enumerate(own_rel):
        start = pl.multiple_of((me ^ rel) * depth, 128)
        own[e] = scratch[:, pl.ds(start, depth)]
        start = pl.multiple_of((me ^ rel ^ 1) * depth, 128)
        sent[e] = scratch[:, pl.ds(start, depth)]


def norm_call(meta, hidden, gain, depth, own_rel):
    rows, width = hidden.shape
    shape = jax.ShapeDtypeStruct((len(own_rel), rows, depth), BF16)
    return pl.pallas_call(
        lambda *refs: norm_body(depth, own_rel, *refs),
        out_shape=(shape, shape),
        in_specs=[
            pl.BlockSpec(memory_space=SMEM),
            pl.BlockSpec(memory_space=pltpu.VMEM),
            pl.BlockSpec(memory_space=pltpu.VMEM),
        ],
        out_specs=(pl.BlockSpec(memory_space=pltpu.VMEM), pl.BlockSpec(memory_space=pltpu.VMEM)),
        scratch_shapes=[pltpu.VMEM((rows, width), BF16)],
        compiler_params=params(),
        cost_estimate=cost(),
        name="layer_norm",
    )(meta, hidden, gain)


def load_weights(refs):
    return [ref[:, 0].reshape(-1, ref.shape[-1]) for ref in refs]


def product(xs, ws, total):
    half = total.shape[0] // 2
    streams = len(xs) // 2
    for core in (0, 1):
        result = None
        k = 0
        for x in xs[core * streams : (core + 1) * streams]:
            for e in range(x.shape[0]):
                term = dot(x[e].reshape(-1, x.shape[-1]), ws[k])
                result = term if result is None else result + term
                k += 1
        total[core * half : (core + 1) * half] = result.astype(total.dtype)


def whole(x):
    nd = len(x.shape)
    return pl.BlockSpec(x.shape, lambda *_: (0,) * nd)


def by_step(x, first=0):
    nd = len(x.shape) - 1
    return pl.BlockSpec((1,) + tuple(x.shape[1:]), lambda i, *_: (first + i,) + (0,) * nd)


def weight_specs(ws, first):
    return [pl.BlockSpec((w.shape[0], 1) + w.shape[2:], lambda i, *_: (0, first + i, 0, 0)) for w in ws]


def partner_body(inputs, *refs):
    product(refs[:inputs], load_weights(refs[inputs:-1]), refs[-1].at[0])


def partner_call(xs, ws, rows, at, heads=1):
    out = jax.ShapeDtypeStruct((heads, rows, ws[0].shape[-1]), BF16)
    return pl.pallas_call(
        lambda *refs: partner_body(len(xs), *refs),
        grid=(heads,),
        out_shape=out,
        in_specs=[whole(x) for x in xs] + weight_specs(ws, at),
        out_specs=by_step(out),
        compiler_params=params(),
        cost_estimate=cost(),
        name="partner_product",
    )(*xs, *ws)


def finish_body(inputs, cap, order_h, order_t, meta, lengths, owners, *refs):
    xs, ws = refs[:inputs], load_weights(refs[inputs:-10])
    arrived, cosine, sine, cache, query, kv, placed, total, slots, counts = refs[-10:]
    me, tp, hg = meta[0], meta[1], meta[2]
    product(xs, ws, total)
    hd = query.shape[2]
    members = [(h, t) for h in order_h for t in order_t]
    run_rows = total.shape[0] // len(members)
    lane = lax.broadcasted_iota(jnp.int32, (run_rows, hd), 1)
    half_rot = ROT // 2
    for m, (rel_h, rel_t) in enumerate(members):
        rows = slice(m * run_rows, (m + 1) * run_rows)
        start = pl.multiple_of(((hg ^ rel_h) * len(order_t) + (tp ^ rel_t)) * run_rows, run_rows)
        to = pl.ds(start, run_rows)
        cos_rows, sin_rows = cosine[to], sine[to]

        def summed(low):
            return total[rows, low : low + hd] + arrived[0, rows, low : low + hd].astype(F32)

        def rotated(part):
            other = jnp.where(
                lane < half_rot, pltpu.roll(part, hd - half_rot, 1), pltpu.roll(part, half_rot, 1)
            )
            return (part * cos_rows + other * sin_rows).astype(BF16)

        query[0, to] = rotated(summed(0))
        kv[0, to, :hd] = rotated(summed(hd))
        kv[0, to, hd:] = summed(2 * hd).astype(BF16)
    owner_count = placed.shape[0]
    blocks = owners.shape[1]
    cached_blocks = lengths[me] // BLOCK
    valid_end = cached_blocks + query.shape[1] // BLOCK
    for s in range(owner_count * cap):
        slots[s] = -1
    for o in range(owner_count):
        counts[o] = 0
    for b in range(blocks):

        @pl.when(b < valid_end)
        def _():
            owner = owners[me, b]
            rank = counts[owner]

            @pl.when(rank < cap)
            def _():
                slots[owner * cap + rank] = b

            counts[owner] = rank + 1

    for s in range(owner_count * cap):
        block = slots[s]
        o, c = divmod(s, cap)

        @pl.when(block < 0)
        def _():
            placed[o, 0, c] = jnp.zeros(placed.shape[3:], BF16)

        @pl.when((block >= 0) & (block < cached_blocks))
        def _():
            at = pl.multiple_of(block * BLOCK, BLOCK)
            placed[o, 0, c] = cache[0, 0, pl.ds(at, BLOCK)]

        @pl.when(block >= cached_blocks)
        def _():
            at = pl.multiple_of((block - cached_blocks) * BLOCK, BLOCK)
            placed[o, 0, c] = kv[0, pl.ds(at, BLOCK)]


def cache_by_step(cache, first):
    return pl.BlockSpec((1, 1) + cache.shape[2:], lambda i, meta, *_: (0, meta[3] + first + i, 0, 0))


def finish_call(meta, lengths, owners, xs, ws, arrived, cosine, sine, cache, at, first, cap, owner_count, orders):
    heads, rows, width = arrived.shape
    hd = width // 3
    cache_spec = cache_by_step(cache, first)
    outs = [(heads, rows, hd), (heads, rows, 2 * hd), (owner_count, heads, cap, BLOCK, 2 * hd)]
    outs = tuple(jax.ShapeDtypeStruct(o, BF16) for o in outs)
    placed_spec = pl.BlockSpec((owner_count, 1, cap, BLOCK, 2 * hd), lambda i, *_: (0, i, 0, 0, 0))
    return pl.pallas_call(
        lambda *refs: finish_body(len(xs), cap, *orders, *refs),
        out_shape=outs,
        grid_spec=pltpu.PrefetchScalarGridSpec(
            num_scalar_prefetch=3,
            grid=(heads,),
            in_specs=[whole(x) for x in xs]
            + weight_specs(ws, at)
            + [by_step(arrived), whole(cosine), whole(sine), cache_spec],
            out_specs=(by_step(outs[0]), by_step(outs[1]), placed_spec),
            scratch_shapes=[
                pltpu.VMEM((rows, width), F32),
                pltpu.SMEM((owner_count * cap,), jnp.int32),
                pltpu.SMEM((owner_count,), jnp.int32),
            ],
        ),
        compiler_params=params(),
        cost_estimate=cost(),
        name="finish_projection",
    )(meta, lengths, owners, *xs, *ws, arrived, cosine, sine, cache)


def attend_body(q_rows, meta, lengths, query, kv, cache, out):
    hd = query.shape[2]
    length = lengths[meta[0]]
    factor = math.log2(math.e) / math.sqrt(hd)
    old_col = lax.broadcasted_iota(jnp.int32, (q_rows, cache.shape[2]), 1)
    causal = lax.broadcasted_iota(jnp.int32, (q_rows, q_rows), 1) <= lax.broadcasted_iota(
        jnp.int32, (q_rows, q_rows), 0
    )
    for step in range(query.shape[1] // q_rows):
        first = step * q_rows
        q = query[0, first : first + q_rows]
        old = jnp.where(old_col < length, dot_t(q, cache[0, 0, :, :hd]), -jnp.inf)
        diag = jnp.where(causal, dot_t(q, kv[0, first : first + q_rows, :hd]), -jnp.inf)
        top = jnp.maximum(jnp.max(old, axis=1, keepdims=True), jnp.max(diag, axis=1, keepdims=True))
        if step:
            new = dot_t(q, kv[0, :first, :hd])
            top = jnp.maximum(top, jnp.max(new, axis=1, keepdims=True))
        old = jnp.exp2((old - top) * factor)
        diag = jnp.exp2((diag - top) * factor)
        total = jnp.sum(old, axis=1, keepdims=True) + jnp.sum(diag, axis=1, keepdims=True)
        result = dot(old.astype(BF16), cache[0, 0, :, hd:]) + dot(diag.astype(BF16), kv[0, first : first + q_rows, hd:])
        if step:
            new = jnp.exp2((new - top) * factor)
            total = total + jnp.sum(new, axis=1, keepdims=True)
            result = result + dot(new.astype(BF16), kv[0, :first, hd:])
        out[0, first : first + q_rows] = (result / total).astype(BF16)


def attend_call(meta, lengths, query, kv, cache, first, q_rows=256):
    heads, rows, hd = query.shape
    out = jax.ShapeDtypeStruct((heads, rows, hd), BF16)
    return pl.pallas_call(
        lambda *refs: attend_body(q_rows, *refs),
        out_shape=out,
        grid_spec=pltpu.PrefetchScalarGridSpec(
            num_scalar_prefetch=2,
            grid=(heads,),
            in_specs=[by_step(query), by_step(kv), cache_by_step(cache, first)],
            out_specs=by_step(out),
        ),
        compiler_params=params(),
        cost_estimate=cost(),
        name="attention",
    )(meta, lengths, query, kv, cache)


def split_body(order_t, meta, *refs):
    held, outs = refs[: -len(order_t)], refs[-len(order_t) :]
    cols = outs[0].shape[-1]
    for r, out in zip(order_t, outs):
        start = pl.multiple_of((meta[1] ^ r) * cols, cols)
        for d, ref in enumerate(held):
            out[d] = ref[:, :, pl.ds(start, cols)]


def split_call(meta, held, order_t):
    heads, hd, width = held[0].shape
    cols = width // len(order_t)
    if cols % 128:
        stacked = jnp.stack(held).reshape(len(held), heads, hd, len(order_t), cols)
        return [lax.dynamic_index_in_dim(stacked, meta[1] ^ r, 3, keepdims=False) for r in order_t]
    vmem = pl.BlockSpec(memory_space=pltpu.VMEM)
    return pl.pallas_call(
        lambda *refs: split_body(order_t, *refs),
        out_shape=[jax.ShapeDtypeStruct((len(held), heads, hd, cols), BF16) for _ in order_t],
        in_specs=[pl.BlockSpec(memory_space=SMEM)] + [vmem] * len(held),
        out_specs=[vmem] * len(order_t),
        compiler_params=params(),
        cost_estimate=cost(),
        name="split_columns",
    )(meta, *held)


def output_body(first, heads, group, order_h, order_t, with_sum, spread, meta, *refs):
    pieces = len(order_h) * len(order_t)
    parts, weights = refs[: 2 * heads], refs[2 * heads : 2 * heads + len(order_t)]
    rest = refs[2 * heads + len(order_t) :]
    tp, hg = meta[1], meta[2]
    total = rest[0][...] if with_sum else None
    for j in range(heads):
        left, right = [], []
        for i, rel_h in enumerate(order_h):
            core, h = divmod(i, len(order_h) // 2)
            for t in range(len(order_t)):
                left.append(parts[2 * j + core][h, t])
                head = (hg ^ rel_h) * group + first + j
                right.append(jnp.concatenate([weights[t][d, head] for d in range(weights[t].shape[0])], axis=1))
        term = dot(jnp.concatenate(left, axis=1), jnp.concatenate(right, axis=0))
        total = term if total is None else total + term
    if not spread:
        rest[-1][...] = total
        return
    scratch, outs = rest[-1], rest[-1 - pieces : -1]
    scratch[...] = total
    run_rows = outs[0].shape[0]
    for i, rel_h in enumerate(order_h):
        for t, rel_t in enumerate(order_t):
            start = pl.multiple_of(((hg ^ rel_h) * len(order_t) + (tp ^ rel_t)) * run_rows, run_rows)
            outs[i * len(order_t) + t][...] = scratch[pl.ds(start, run_rows)].astype(BF16)


def output_call(meta, parts, weights, rows, first, group, order_h, order_t, total=None, spread=False):
    members = len(order_h) * len(order_t)
    dps, cols = weights[0].shape[0], weights[0].shape[-1]
    vmem = pl.BlockSpec(memory_space=pltpu.VMEM)
    operands = (meta, *parts, *weights) + (() if total is None else (total,))
    heads = len(parts) // 2
    out = jax.ShapeDtypeStruct((rows, dps * cols), F32)
    piece = jax.ShapeDtypeStruct((rows // members, dps * cols), BF16)
    return pl.pallas_call(
        lambda *refs: output_body(first, heads, group, order_h, order_t, total is not None, spread, *refs),
        out_shape=[piece] * members if spread else out,
        in_specs=[pl.BlockSpec(memory_space=SMEM)] + [vmem] * (len(operands) - 1),
        out_specs=[vmem] * members if spread else vmem,
        scratch_shapes=[pltpu.VMEM((rows, dps * cols), F32)] if spread else [],
        compiler_params=params(),
        cost_estimate=cost(),
        name="output_projection",
    )(*operands)


def output_plain(place, hg, parts, weights, rows, group, order_h, order_t):
    dps, heads, hd, cols = weights[0].shape
    stacked = jnp.stack(weights).reshape(len(order_t), dps, len(order_h), group, hd, cols)
    stacked = jnp.take(stacked, place, axis=1)
    stacked = jnp.take(stacked, hg ^ jnp.array(order_h, jnp.int32), axis=2)
    total = None
    for j in range(group):
        left = jnp.concatenate([parts[2 * j], parts[2 * j + 1]], axis=0)
        left = left.transpose(2, 0, 1, 3).reshape(rows, -1)
        right = stacked[:, :, :, j].transpose(2, 0, 3, 1, 4).reshape(-1, dps * cols)
        term = dot(left, right)
        total = term if total is None else total + term
    return total.astype(BF16)


def collect_body(count, *refs):
    head = 0
    for piece in refs[:count]:
        for j in range(piece.shape[1]):
            refs[-1][0, head, 0] = piece[0, j]
            head += 1


def collect_call(pieces, heads, first, base=None):
    count = sum(p.shape[1] for p in pieces)
    requests = pieces[0].shape[0]
    tail = pieces[0].shape[2:]
    based = [] if base is None else [base]
    return pl.pallas_call(
        lambda *refs: collect_body(len(pieces), *refs),
        grid=(requests,),
        out_shape=jax.ShapeDtypeStruct((1, heads, requests) + tail, BF16),
        in_specs=[by_step(p) for p in pieces] + [pl.BlockSpec(memory_space=pl.ANY)] * len(based),
        out_specs=pl.BlockSpec((1, count, 1) + tail, lambda r: (0, first // count, r, 0, 0, 0)),
        input_output_aliases={len(pieces): 0} if based else {},
        compiler_params=params(),
        cost_estimate=cost(),
        name="collect_blocks",
    )(*pieces, *based)


def residual_body(order_d, order_h, order_t, meta, hidden, *refs):
    pieces, out = refs[:-1], refs[-1]
    cols = pieces[0].shape[1] // len(order_d)
    nh, nt = len(order_h), len(order_t)
    for i, rel_h in enumerate(order_h):
        for t, rel_t in enumerate(order_t):
            piece = pieces[i * nt + t]
            for d, rel_d in enumerate(order_d):
                start = (((meta[0] ^ rel_d) * nh + (meta[2] ^ rel_h)) * nt + (meta[1] ^ rel_t)) * cols
                at = pl.ds(pl.multiple_of(start, cols), cols)
                summed = piece[:, d * cols : (d + 1) * cols].astype(F32)
                out[:, at] = (hidden[:, at].astype(F32) + summed).astype(BF16)


def residual_call(meta, hidden, pieces, order_d, order_h, order_t):
    vmem = pl.BlockSpec(memory_space=pltpu.VMEM)
    return pl.pallas_call(
        lambda *refs: residual_body(order_d, order_h, order_t, *refs),
        out_shape=jax.ShapeDtypeStruct(hidden.shape, BF16),
        in_specs=[pl.BlockSpec(memory_space=SMEM)] + [vmem] * (1 + len(pieces)),
        out_specs=vmem,
        compiler_params=params(),
        cost_estimate=cost(9),
        name="residual",
    )(meta, hidden, *pieces)


def plane_swap(x, rel_h, rel_t):
    nt, nh = lax.axis_size("tp"), lax.axis_size("hg")
    pairs = [(t * nh + h, (t ^ rel_t) * nh + (h ^ rel_h)) for t in range(nt) for h in range(nh)]
    return lax.ppermute(x, ("tp", "hg"), pairs)


def head_gather(x, h_strides, t_strides, h_first, token=None):
    def over_h(x):
        for s in h_strides[:-1]:
            x = jnp.concatenate([x, swap(x, "hg", s)], axis=0)
        return x

    def over_t(x):
        for s in t_strides:
            x = jnp.concatenate([x, swap(x, "tp", s)], axis=1)
        return x

    first, second = (over_h, over_t) if h_first else (over_t, over_h)
    x = second(first(x[None, None]))
    if token is not None:
        x = after(x, token)
    return [x, swap(x, "hg", h_strides[-1])]


def plan_of(group):
    if group % 4 == 0:
        q = group // 4
        return [2 * q, 2 * q], [(0, q, 2, 3), (q, q, 3, 4), (2 * q, 2 * q, 4, 4)]
    return [group], [(0, group, 3, 3)]


def on_device(hidden_in, norm_gain, qkv_weight, out_weight, cache_kv, cached_lengths, owner_table):
    nt, nh, nd = lax.axis_size("tp"), lax.axis_size("hg"), lax.axis_size("dp")
    tp, hg, dp = lax.axis_index("tp"), lax.axis_index("hg"), lax.axis_index("dp")
    local_rows, width = hidden_in.shape[2:]
    local_depth, _, local_heads, hd = qkv_weight.shape
    group = local_heads // nh
    depth = local_depth * nh
    rows = local_rows * nt * nh
    cap = (cache_kv.shape[2] + rows) // BLOCK // nd
    length = lax.dynamic_index_in_dim(cached_lengths, dp, 0, keepdims=False)

    far, all_d = halving(nd, 2), halving(nd, 1)
    own_rel = offsets(far)
    h_strides, t_strides = halving(nh, 1), halving(nt, 1)
    order_h, order_t = offsets(h_strides), offsets(t_strides)
    members = dp ^ jnp.arange(nd, dtype=jnp.int32)
    place = sum(jnp.where(members == rel, k, 0) for k, rel in enumerate(offsets(all_d))).astype(jnp.int32)
    meta = jnp.stack([dp, tp, hg, hg * group]).astype(jnp.int32)

    cols = out_weight.shape[2] // nt
    out_held = [out_weight]
    for s in far[:-1]:
        out_held = out_held + [swap(w, "dp", s) for w in out_held]
    *come, out_near = hold([swap(w, "dp", far[-1]) for w in out_held] + [swap(out_weight, "dp", 1)], 60)
    out_held = out_held + come
    by_head = qkv_weight.reshape(local_depth, 3, nh, group, hd).transpose(2, 3, 0, 1, 4)
    by_head = by_head.reshape(nh, group, local_depth, 3 * hd)
    sizes, finishing = plan_of(group)
    firsts = [sum(sizes[:c]) for c in range(len(sizes))]
    given = [by_head[:, f : f + size] for f, size in zip(firsts, sizes)]
    mine = [lax.all_to_all(given[0], "hg", 0, 0, tiled=True)]

    def over_h(x):
        for s in h_strides[:-1]:
            x = jnp.concatenate([x, swap(x, "hg", s)], axis=1)
        return x

    def over_t(x):
        for s in t_strides:
            x = jnp.concatenate([x, swap(x, "tp", s)], axis=2)
        return x

    own, sent = norm_call(meta, after(hidden_in[0, 0], given[0]), norm_gain.reshape(1, width), depth, own_rel)
    cut = len(own_rel) // 2
    own, pair = own[:, None, None], swap(sent, "dp", 1)[:, None, None]
    own = [over_t(over_h(own[:cut])), over_h(over_t(own[cut:]))]
    pair = [pair[:cut], pair[cut:]]

    positions = length + jnp.arange(rows, dtype=jnp.int32)
    half_rot = ROT // 2
    frequency = 10000.0 ** (-2.0 * jnp.arange(half_rot, dtype=F32) / ROT)
    angles = positions.astype(F32)[:, None] * frequency[None, :]
    cos_half, sin_half = jnp.cos(angles), jnp.sin(angles)
    cosine = jnp.concatenate([cos_half, cos_half, jnp.ones((rows, hd - ROT), F32)], axis=1)
    sine = jnp.concatenate([-sin_half, sin_half, jnp.zeros((rows, hd - ROT), F32)], axis=1)
    live = dict(out=out_held, near=out_near, mine=mine, given=given[1:], own=own, pair=pair)
    live["tables"] = (cosine, sine)
    live = lax.optimization_barrier(live)

    weights, arrived, ready, placed = [], {}, {}, {}
    handed, gathered = {}, {}
    chunks = len(sizes)
    places = [(c, i) for c, size in enumerate(sizes) for i in range(size)]
    last_stage = chunks + 2
    for stage in range(1, last_stage + 1):
        if stage <= chunks:
            held = [live["mine"][stage - 1]]
            for s in far[:-1]:
                held = held + [swap(w, "dp", s) for w in held]
            come = [swap(w, "dp", far[-1]) for w in held]
            with_out = [swap(w, "dp", 1) for w in live["out"][1:]] if stage == 1 else []
            come = hold(come + with_out, 150)
            weights.append(held + come[: len(held)])
            if stage == 1:
                live["out"] = live["out"] + [live.pop("near")] + come[len(held) :]
        if stage == 1:
            live["mine"] = live["mine"] + [lax.all_to_all(g, "hg", 0, 0, tiled=True) for g in live.pop("given")]
            pair = [over_t(over_h(live["pair"][0])), over_h(over_t(live["pair"][1]))]
            live["pair"] = pair + [swap(x, "hg", h_strides[-1]) for x in pair]
            own = after(live["own"], tuple(live["pair"]))
            live["own"] = own + [swap(x, "hg", h_strides[-1]) for x in own]
        moved = [f for f, _, at, handover in finishing if at < handover == stage]
        come = [lax.all_to_all(live["placed"][f], "dp", 0, 0, tiled=True) for f in moved]
        sent = []
        for first, count, at, _ in finishing:
            c, i = places[first]
            if c + 2 == stage:
                partial = partner_call(live["pair"], live["weights"][c], rows, i, count)
                arrived[first] = swap(partial, "dp", 1)
                sent.append(first)
        if stage == chunks + 1:
            come = hold(come + [arrived[f] for f in sent], 60)
            arrived.update(zip(sent, come[len(moved) :]))
        handed.update(zip(moved, come))
        if stage == 2:
            held = split_call(meta, after(live["out"], partial), order_t)
            live["out"] = [swap(w, "tp", r) if r else w for w, r in zip(held, order_t)]
        for first, count, at, _ in finishing:
            if at == stage - 1 and first not in gathered:
                gathered[first] = [
                    head_gather(after(live["ready"][first], partial)[i], h_strides, t_strides, i % 2 == 0)
                    for i in range(count)
                ]
        for first, count, at, handover in finishing:
            if at == stage:
                c, i = places[first]
                come = live["arrived"].get(first)
                come = arrived[first] if come is None else come
                if 2 < at < last_stage:
                    come = after(come, partial)
                query, kv, placed[first] = finish_call(
                    meta, cached_lengths, owner_table, live["own"], live["weights"][c], come,
                    *live["tables"], cache_kv, i, first, cap, nd, (order_h, order_t),
                )
                ready[first] = attend_call(meta, cached_lengths, query, kv, cache_kv, first)
                if 2 < at < last_stage:
                    gathered[first] = [
                        head_gather(ready[first][n], h_strides, t_strides, n % 2 == 1) for n in range(count)
                    ]
                if at == handover:
                    blocks = after(placed[first], ready[first])
                    handed[first] = lax.all_to_all(blocks, "dp", 0, 0, tiled=True)
        if stage == last_stage:
            break
        live.update(weights=weights, arrived=arrived, ready=ready, placed=placed, handed=handed, gathered=gathered)
        live = lax.optimization_barrier(live)
        weights = list(live["weights"])
        arrived, ready, placed = dict(live["arrived"]), dict(live["ready"]), dict(live["placed"])
        handed, gathered = dict(live["handed"]), dict(live["gathered"])

    out_weights = live["out"]
    first, count, _, _ = finishing[-1]
    done = sorted(gathered)
    summed = None
    if done and cols % 128 == 0:
        parts = [p for f in done for head in gathered[f] for p in head]
        summed = output_call(meta, parts, out_weights, rows, 0, group, order_h, order_t)
    gathered[first] = [
        head_gather(ready[first][i], h_strides, t_strides, i % 2 == 0, summed) for i in range(count)
    ]
    collected = None
    if cols % 128 == 0:
        parts = [p for head in gathered[first] for p in head]
        pieces = output_call(meta, parts, out_weights, rows, first, group, order_h, order_t, summed, True)
        rels = [(h, t) for h in order_h for t in order_t]
        pieces = [plane_swap(p, h, t) if h or t else p for p, (h, t) in zip(pieces, rels)]
        if 2 * count == group:
            early = [handed[f] for f, _, _, _ in finishing[:-1]]
            collected = collect_call(early, group, 0)
            pieces[0] = after(pieces[0], collected)
        hidden_out = residual_call(meta, hidden_in[0, 0], pieces, offsets(all_d), order_h, order_t)
    else:
        parts = [p for f in sorted(gathered) for head in gathered[f] for p in head]
        summed = output_plain(place, hg, parts, out_weights, rows, group, order_h, order_t)
        summed = lax.all_to_all(
            summed.reshape(nh * nt, local_rows, nd * cols), ("hg", "tp"), 0, 0, tiled=True
        )
        summed = summed.reshape(nh, nt, local_rows, nd, cols).transpose(2, 3, 0, 1, 4).reshape(local_rows, width)
        hidden_out = (hidden_in[0, 0].astype(F32) + summed.astype(F32)).astype(BF16)
    if collected is not None:
        collected = collect_call([handed[first]], group, first, collected)
    else:
        collected = collect_call([handed[f] for f, _, _, _ in finishing], group, 0)
    return hidden_out[None, None], collected


def solution(mesh):
    return jax.shard_map(
        on_device,
        mesh=mesh,
        in_specs=(
            P("dp", "hg", "tp", None),
            P(),
            P(("dp", "hg"), None, "tp", None),
            P("tp", None, ("dp", "hg")),
            P("dp", "tp", None, None),
            P(),
            P(),
        ),
        out_specs=(P("dp", "hg", "tp", None), P("dp", ("tp", "hg"), None, None, None, None)),
        check_vma=False,
    )
```

```python
import math

import jax
import jax.numpy as jnp
from jax import lax
from jax.experimental import pallas as pl
from jax.experimental.pallas import tpu as pltpu
from jax.sharding import PartitionSpec as P

ROT = 32
BLOCK = 128
EPSILON = 1e-05
VMEM_LIMIT = 48 * 1024 * 1024

SMEM = pltpu.SMEM
BF16 = jnp.bfloat16
F32 = jnp.float32


def params():
    return pltpu.CompilerParams(vmem_limit_bytes=VMEM_LIMIT)


def cost(microseconds=0):
    return pl.CostEstimate(flops=1 + int(microseconds * 1e9), bytes_accessed=1, transcendentals=0)


def hold(xs, microseconds):
    hbm = pl.BlockSpec(memory_space=pl.ANY)
    held = pl.pallas_call(
        lambda *refs: None,
        out_shape=[jax.ShapeDtypeStruct(x.shape, x.dtype) for x in xs],
        in_specs=[hbm] * len(xs),
        out_specs=[hbm] * len(xs),
        input_output_aliases={i: i for i in range(len(xs))},
        cost_estimate=pl.CostEstimate(flops=int(microseconds * 1e9), bytes_accessed=1, transcendentals=0),
        name="hold",
    )(*xs)
    return list(held)


def swap(x, axis, stride):
    size = lax.axis_size(axis)
    return lax.ppermute(x, axis, [(i, i ^ stride) for i in range(size)])


def halving(size, last):
    strides = []
    step = size // 2
    while step >= last:
        strides.append(step)
        step //= 2
    return strides


def offsets(strides):
    order = [0]
    for stride in strides:
        order = order + [o ^ stride for o in order]
    return order


def after(value, token):
    return lax.optimization_barrier((value, token))[0]


def dot(a, b):
    return jnp.dot(a, b, preferred_element_type=F32)


def dot_t(a, b):
    return lax.dot_general(a, b, (((1,), (1,)), ((), ())), preferred_element_type=F32)


def norm_body(depth, own_rel, meta, hidden, gain, own, sent, scratch):
    rows = hidden[...].astype(F32)
    centered = rows - jnp.mean(rows, axis=-1, keepdims=True)
    spread = jnp.mean(centered * centered, axis=-1, keepdims=True)
    scratch[...] = (centered * lax.rsqrt(spread + EPSILON) * gain[...]).astype(BF16)
    me = meta[0]
    for e, rel in enumerate(own_rel):
        start = pl.multiple_of((me ^ rel) * depth, 128)
        own[e] = scratch[:, pl.ds(start, depth)]
        start = pl.multiple_of((me ^ rel ^ 1) * depth, 128)
        sent[e] = scratch[:, pl.ds(start, depth)]


def norm_call(meta, hidden, gain, depth, own_rel):
    rows, width = hidden.shape
    shape = jax.ShapeDtypeStruct((len(own_rel), rows, depth), BF16)
    return pl.pallas_call(
        lambda *refs: norm_body(depth, own_rel, *refs),
        out_shape=(shape, shape),
        in_specs=[
            pl.BlockSpec(memory_space=SMEM),
            pl.BlockSpec(memory_space=pltpu.VMEM),
            pl.BlockSpec(memory_space=pltpu.VMEM),
        ],
        out_specs=(pl.BlockSpec(memory_space=pltpu.VMEM), pl.BlockSpec(memory_space=pltpu.VMEM)),
        scratch_shapes=[pltpu.VMEM((rows, width), BF16)],
        compiler_params=params(),
        cost_estimate=cost(),
        name="layer_norm",
    )(meta, hidden, gain)


def load_weights(refs):
    return [ref[:, 0].reshape(-1, ref.shape[-1]) for ref in refs]


def product(xs, ws, total):
    half = total.shape[0] // 2
    streams = len(xs) // 2
    for core in (0, 1):
        result = None
        k = 0
        for x in xs[core * streams : (core + 1) * streams]:
            for e in range(x.shape[0]):
                term = dot(x[e].reshape(-1, x.shape[-1]), ws[k])
                result = term if result is None else result + term
                k += 1
        total[core * half : (core + 1) * half] = result.astype(total.dtype)


def whole(x):
    nd = len(x.shape)
    return pl.BlockSpec(x.shape, lambda *_: (0,) * nd)


def by_step(x, first=0):
    nd = len(x.shape) - 1
    return pl.BlockSpec((1,) + tuple(x.shape[1:]), lambda i, *_: (first + i,) + (0,) * nd)


def weight_specs(ws, first):
    return [pl.BlockSpec((w.shape[0], 1) + w.shape[2:], lambda i, *_: (0, first + i, 0, 0)) for w in ws]


def partner_body(inputs, *refs):
    product(refs[:inputs], load_weights(refs[inputs:-1]), refs[-1].at[0])


def partner_call(xs, ws, rows, at, heads=1):
    out = jax.ShapeDtypeStruct((heads, rows, ws[0].shape[-1]), BF16)
    return pl.pallas_call(
        lambda *refs: partner_body(len(xs), *refs),
        grid=(heads,),
        out_shape=out,
        in_specs=[whole(x) for x in xs] + weight_specs(ws, at),
        out_specs=by_step(out),
        compiler_params=params(),
        cost_estimate=cost(),
        name="partner_product",
    )(*xs, *ws)


def finish_body(inputs, cap, order_h, order_t, meta, lengths, owners, *refs):
    xs, ws = refs[:inputs], load_weights(refs[inputs:-10])
    arrived, cosine, sine, cache, query, kv, placed, total, slots, counts = refs[-10:]
    me, tp, hg = meta[0], meta[1], meta[2]
    product(xs, ws, total)
    hd = query.shape[2]
    members = [(h, t) for h in order_h for t in order_t]
    run_rows = total.shape[0] // len(members)
    lane = lax.broadcasted_iota(jnp.int32, (run_rows, hd), 1)
    half_rot = ROT // 2
    for m, (rel_h, rel_t) in enumerate(members):
        rows = slice(m * run_rows, (m + 1) * run_rows)
        start = pl.multiple_of(((hg ^ rel_h) * len(order_t) + (tp ^ rel_t)) * run_rows, run_rows)
        to = pl.ds(start, run_rows)
        cos_rows, sin_rows = cosine[to], sine[to]

        def summed(low):
            return total[rows, low : low + hd] + arrived[0, rows, low : low + hd].astype(F32)

        def rotated(part):
            other = jnp.where(
                lane < half_rot, pltpu.roll(part, hd - half_rot, 1), pltpu.roll(part, half_rot, 1)
            )
            return (part * cos_rows + other * sin_rows).astype(BF16)

        query[0, to] = rotated(summed(0))
        kv[0, to, :hd] = rotated(summed(hd))
        kv[0, to, hd:] = summed(2 * hd).astype(BF16)
    owner_count = placed.shape[0]
    blocks = owners.shape[1]
    cached_blocks = lengths[me] // BLOCK
    valid_end = cached_blocks + query.shape[1] // BLOCK
    for s in range(owner_count * cap):
        slots[s] = -1
    for o in range(owner_count):
        counts[o] = 0
    for b in range(blocks):

        @pl.when(b < valid_end)
        def _():
            owner = owners[me, b]
            rank = counts[owner]

            @pl.when(rank < cap)
            def _():
                slots[owner * cap + rank] = b

            counts[owner] = rank + 1

    for s in range(owner_count * cap):
        block = slots[s]
        o, c = divmod(s, cap)

        @pl.when(block < 0)
        def _():
            placed[o, 0, c] = jnp.zeros(placed.shape[3:], BF16)

        @pl.when((block >= 0) & (block < cached_blocks))
        def _():
            at = pl.multiple_of(block * BLOCK, BLOCK)
            placed[o, 0, c] = cache[0, 0, pl.ds(at, BLOCK)]

        @pl.when(block >= cached_blocks)
        def _():
            at = pl.multiple_of((block - cached_blocks) * BLOCK, BLOCK)
            placed[o, 0, c] = kv[0, pl.ds(at, BLOCK)]


def cache_by_step(cache, first):
    return pl.BlockSpec((1, 1) + cache.shape[2:], lambda i, meta, *_: (0, meta[3] + first + i, 0, 0))


def finish_call(meta, lengths, owners, xs, ws, arrived, cosine, sine, cache, at, first, cap, owner_count, orders):
    heads, rows, width = arrived.shape
    hd = width // 3
    cache_spec = cache_by_step(cache, first)
    outs = [(heads, rows, hd), (heads, rows, 2 * hd), (owner_count, heads, cap, BLOCK, 2 * hd)]
    outs = tuple(jax.ShapeDtypeStruct(o, BF16) for o in outs)
    placed_spec = pl.BlockSpec((owner_count, 1, cap, BLOCK, 2 * hd), lambda i, *_: (0, i, 0, 0, 0))
    return pl.pallas_call(
        lambda *refs: finish_body(len(xs), cap, *orders, *refs),
        out_shape=outs,
        grid_spec=pltpu.PrefetchScalarGridSpec(
            num_scalar_prefetch=3,
            grid=(heads,),
            in_specs=[whole(x) for x in xs]
            + weight_specs(ws, at)
            + [by_step(arrived), whole(cosine), whole(sine), cache_spec],
            out_specs=(by_step(outs[0]), by_step(outs[1]), placed_spec),
            scratch_shapes=[
                pltpu.VMEM((rows, width), F32),
                pltpu.SMEM((owner_count * cap,), jnp.int32),
                pltpu.SMEM((owner_count,), jnp.int32),
            ],
        ),
        compiler_params=params(),
        cost_estimate=cost(),
        name="finish_projection",
    )(meta, lengths, owners, *xs, *ws, arrived, cosine, sine, cache)


def attend_body(q_rows, meta, lengths, query, kv, cache, out):
    hd = query.shape[2]
    length = lengths[meta[0]]
    factor = math.log2(math.e) / math.sqrt(hd)
    old_col = lax.broadcasted_iota(jnp.int32, (q_rows, cache.shape[2]), 1)
    causal = lax.broadcasted_iota(jnp.int32, (q_rows, q_rows), 1) <= lax.broadcasted_iota(
        jnp.int32, (q_rows, q_rows), 0
    )
    for step in range(query.shape[1] // q_rows):
        first = step * q_rows
        q = query[0, first : first + q_rows]
        old = jnp.where(old_col < length, dot_t(q, cache[0, 0, :, :hd]), -jnp.inf)
        diag = jnp.where(causal, dot_t(q, kv[0, first : first + q_rows, :hd]), -jnp.inf)
        top = jnp.maximum(jnp.max(old, axis=1, keepdims=True), jnp.max(diag, axis=1, keepdims=True))
        if step:
            new = dot_t(q, kv[0, :first, :hd])
            top = jnp.maximum(top, jnp.max(new, axis=1, keepdims=True))
        old = jnp.exp2((old - top) * factor)
        diag = jnp.exp2((diag - top) * factor)
        total = jnp.sum(old, axis=1, keepdims=True) + jnp.sum(diag, axis=1, keepdims=True)
        result = dot(old.astype(BF16), cache[0, 0, :, hd:]) + dot(diag.astype(BF16), kv[0, first : first + q_rows, hd:])
        if step:
            new = jnp.exp2((new - top) * factor)
            total = total + jnp.sum(new, axis=1, keepdims=True)
            result = result + dot(new.astype(BF16), kv[0, :first, hd:])
        out[0, first : first + q_rows] = (result / total).astype(BF16)


def attend_call(meta, lengths, query, kv, cache, first, q_rows=256):
    heads, rows, hd = query.shape
    out = jax.ShapeDtypeStruct((heads, rows, hd), BF16)
    return pl.pallas_call(
        lambda *refs: attend_body(q_rows, *refs),
        out_shape=out,
        grid_spec=pltpu.PrefetchScalarGridSpec(
            num_scalar_prefetch=2,
            grid=(heads,),
            in_specs=[by_step(query), by_step(kv), cache_by_step(cache, first)],
            out_specs=by_step(out),
        ),
        compiler_params=params(),
        cost_estimate=cost(),
        name="attention",
    )(meta, lengths, query, kv, cache)


def split_body(order_t, meta, *refs):
    held, outs = refs[: -len(order_t)], refs[-len(order_t) :]
    cols = outs[0].shape[-1]
    for r, out in zip(order_t, outs):
        start = pl.multiple_of((meta[1] ^ r) * cols, cols)
        for d, ref in enumerate(held):
            out[d] = ref[:, :, pl.ds(start, cols)]


def split_call(meta, held, order_t):
    heads, hd, width = held[0].shape
    cols = width // len(order_t)
    if cols % 128:
        stacked = jnp.stack(held).reshape(len(held), heads, hd, len(order_t), cols)
        return [lax.dynamic_index_in_dim(stacked, meta[1] ^ r, 3, keepdims=False) for r in order_t]
    vmem = pl.BlockSpec(memory_space=pltpu.VMEM)
    return pl.pallas_call(
        lambda *refs: split_body(order_t, *refs),
        out_shape=[jax.ShapeDtypeStruct((len(held), heads, hd, cols), BF16) for _ in order_t],
        in_specs=[pl.BlockSpec(memory_space=SMEM)] + [vmem] * len(held),
        out_specs=[vmem] * len(order_t),
        compiler_params=params(),
        cost_estimate=cost(),
        name="split_columns",
    )(meta, *held)


def output_body(first, heads, group, order_h, order_t, with_sum, spread, meta, *refs):
    pieces = len(order_h) * len(order_t)
    parts, weights = refs[: 2 * heads], refs[2 * heads : 2 * heads + len(order_t)]
    rest = refs[2 * heads + len(order_t) :]
    tp, hg = meta[1], meta[2]
    total = rest[0][...] if with_sum else None
    for j in range(heads):
        left, right = [], []
        for i, rel_h in enumerate(order_h):
            core, h = divmod(i, len(order_h) // 2)
            for t in range(len(order_t)):
                left.append(parts[2 * j + core][h, t])
                head = (hg ^ rel_h) * group + first + j
                right.append(jnp.concatenate([weights[t][d, head] for d in range(weights[t].shape[0])], axis=1))
        term = dot(jnp.concatenate(left, axis=1), jnp.concatenate(right, axis=0))
        total = term if total is None else total + term
    if not spread:
        rest[-1][...] = total
        return
    scratch, outs = rest[-1], rest[-1 - pieces : -1]
    scratch[...] = total
    run_rows = outs[0].shape[0]
    for i, rel_h in enumerate(order_h):
        for t, rel_t in enumerate(order_t):
            start = pl.multiple_of(((hg ^ rel_h) * len(order_t) + (tp ^ rel_t)) * run_rows, run_rows)
            outs[i * len(order_t) + t][...] = scratch[pl.ds(start, run_rows)].astype(BF16)


def output_call(meta, parts, weights, rows, first, group, order_h, order_t, total=None, spread=False):
    members = len(order_h) * len(order_t)
    dps, cols = weights[0].shape[0], weights[0].shape[-1]
    vmem = pl.BlockSpec(memory_space=pltpu.VMEM)
    operands = (meta, *parts, *weights) + (() if total is None else (total,))
    heads = len(parts) // 2
    out = jax.ShapeDtypeStruct((rows, dps * cols), F32)
    piece = jax.ShapeDtypeStruct((rows // members, dps * cols), BF16)
    return pl.pallas_call(
        lambda *refs: output_body(first, heads, group, order_h, order_t, total is not None, spread, *refs),
        out_shape=[piece] * members if spread else out,
        in_specs=[pl.BlockSpec(memory_space=SMEM)] + [vmem] * (len(operands) - 1),
        out_specs=[vmem] * members if spread else vmem,
        scratch_shapes=[pltpu.VMEM((rows, dps * cols), F32)] if spread else [],
        compiler_params=params(),
        cost_estimate=cost(),
        name="output_projection",
    )(*operands)


def output_plain(place, hg, parts, weights, rows, group, order_h, order_t):
    dps, heads, hd, cols = weights[0].shape
    stacked = jnp.stack(weights).reshape(len(order_t), dps, len(order_h), group, hd, cols)
    stacked = jnp.take(stacked, place, axis=1)
    stacked = jnp.take(stacked, hg ^ jnp.array(order_h, jnp.int32), axis=2)
    total = None
    for j in range(group):
        left = jnp.concatenate([parts[2 * j], parts[2 * j + 1]], axis=0)
        left = left.transpose(2, 0, 1, 3).reshape(rows, -1)
        right = stacked[:, :, :, j].transpose(2, 0, 3, 1, 4).reshape(-1, dps * cols)
        term = dot(left, right)
        total = term if total is None else total + term
    return total.astype(BF16)


def collect_body(count, *refs):
    head = 0
    for piece in refs[:count]:
        for j in range(piece.shape[1]):
            refs[-1][0, head, 0] = piece[0, j]
            head += 1


def collect_call(pieces, heads, first, base=None):
    count = sum(p.shape[1] for p in pieces)
    requests = pieces[0].shape[0]
    tail = pieces[0].shape[2:]
    based = [] if base is None else [base]
    return pl.pallas_call(
        lambda *refs: collect_body(len(pieces), *refs),
        grid=(requests,),
        out_shape=jax.ShapeDtypeStruct((1, heads, requests) + tail, BF16),
        in_specs=[by_step(p) for p in pieces] + [pl.BlockSpec(memory_space=pl.ANY)] * len(based),
        out_specs=pl.BlockSpec((1, count, 1) + tail, lambda r: (0, first // count, r, 0, 0, 0)),
        input_output_aliases={len(pieces): 0} if based else {},
        compiler_params=params(),
        cost_estimate=cost(),
        name="collect_blocks",
    )(*pieces, *based)


def residual_body(order_d, order_h, order_t, meta, hidden, *refs):
    pieces, out = refs[:-1], refs[-1]
    cols = pieces[0].shape[1] // len(order_d)
    nh, nt = len(order_h), len(order_t)
    for i, rel_h in enumerate(order_h):
        for t, rel_t in enumerate(order_t):
            piece = pieces[i * nt + t]
            for d, rel_d in enumerate(order_d):
                start = (((meta[0] ^ rel_d) * nh + (meta[2] ^ rel_h)) * nt + (meta[1] ^ rel_t)) * cols
                at = pl.ds(pl.multiple_of(start, cols), cols)
                summed = piece[:, d * cols : (d + 1) * cols].astype(F32)
                out[:, at] = (hidden[:, at].astype(F32) + summed).astype(BF16)


def residual_call(meta, hidden, pieces, order_d, order_h, order_t):
    vmem = pl.BlockSpec(memory_space=pltpu.VMEM)
    return pl.pallas_call(
        lambda *refs: residual_body(order_d, order_h, order_t, *refs),
        out_shape=jax.ShapeDtypeStruct(hidden.shape, BF16),
        in_specs=[pl.BlockSpec(memory_space=SMEM)] + [vmem] * (1 + len(pieces)),
        out_specs=vmem,
        compiler_params=params(),
        cost_estimate=cost(9),
        name="residual",
    )(meta, hidden, *pieces)


def plane_swap(x, rel_h, rel_t):
    nt, nh = lax.axis_size("tp"), lax.axis_size("hg")
    pairs = [(t * nh + h, (t ^ rel_t) * nh + (h ^ rel_h)) for t in range(nt) for h in range(nh)]
    return lax.ppermute(x, ("tp", "hg"), pairs)


def head_gather(x, h_strides, t_strides, h_first, token=None):
    def over_h(x):
        for s in h_strides[:-1]:
            x = jnp.concatenate([x, swap(x, "hg", s)], axis=0)
        return x

    def over_t(x):
        for s in t_strides:
            x = jnp.concatenate([x, swap(x, "tp", s)], axis=1)
        return x

    first, second = (over_h, over_t) if h_first else (over_t, over_h)
    x = second(first(x[None, None]))
    if token is not None:
        x = after(x, token)
    return [x, swap(x, "hg", h_strides[-1])]


def plan_of(group):
    if group % 4 == 0:
        q = group // 4
        return [2 * q, 2 * q], [(0, q, 2, 3), (q, q, 3, 4), (2 * q, 2 * q, 4, 4)]
    return [group], [(0, group, 3, 3)]


def on_device(hidden_in, norm_gain, qkv_weight, out_weight, cache_kv, cached_lengths, owner_table):
    nt, nh, nd = lax.axis_size("tp"), lax.axis_size("hg"), lax.axis_size("dp")
    tp, hg, dp = lax.axis_index("tp"), lax.axis_index("hg"), lax.axis_index("dp")
    local_rows, width = hidden_in.shape[2:]
    local_depth, _, local_heads, hd = qkv_weight.shape
    group = local_heads // nh
    depth = local_depth * nh
    rows = local_rows * nt * nh
    cap = (cache_kv.shape[2] + rows) // BLOCK // nd
    length = lax.dynamic_index_in_dim(cached_lengths, dp, 0, keepdims=False)

    far, all_d = halving(nd, 2), halving(nd, 1)
    own_rel = offsets(far)
    h_strides, t_strides = halving(nh, 1), halving(nt, 1)
    order_h, order_t = offsets(h_strides), offsets(t_strides)
    members = dp ^ jnp.arange(nd, dtype=jnp.int32)
    place = sum(jnp.where(members == rel, k, 0) for k, rel in enumerate(offsets(all_d))).astype(jnp.int32)
    meta = jnp.stack([dp, tp, hg, hg * group]).astype(jnp.int32)

    cols = out_weight.shape[2] // nt
    out_held = [out_weight]
    for s in far[:-1]:
        out_held = out_held + [swap(w, "dp", s) for w in out_held]
    *come, out_near = hold([swap(w, "dp", far[-1]) for w in out_held] + [swap(out_weight, "dp", 1)], 60)
    out_held = out_held + come
    by_head = qkv_weight.reshape(local_depth, 3, nh, group, hd).transpose(2, 3, 0, 1, 4)
    by_head = by_head.reshape(nh, group, local_depth, 3 * hd)
    sizes, finishing = plan_of(group)
    firsts = [sum(sizes[:c]) for c in range(len(sizes))]
    given = [by_head[:, f : f + size] for f, size in zip(firsts, sizes)]
    mine = [lax.all_to_all(given[0], "hg", 0, 0, tiled=True)]

    def over_h(x):
        for s in h_strides[:-1]:
            x = jnp.concatenate([x, swap(x, "hg", s)], axis=1)
        return x

    def over_t(x):
        for s in t_strides:
            x = jnp.concatenate([x, swap(x, "tp", s)], axis=2)
        return x

    own, sent = norm_call(meta, after(hidden_in[0, 0], given[0]), norm_gain.reshape(1, width), depth, own_rel)
    cut = len(own_rel) // 2
    own, pair = own[:, None, None], swap(sent, "dp", 1)[:, None, None]
    own = [over_t(over_h(own[:cut])), over_h(over_t(own[cut:]))]
    pair = [pair[:cut], pair[cut:]]

    positions = length + jnp.arange(rows, dtype=jnp.int32)
    half_rot = ROT // 2
    frequency = 10000.0 ** (-2.0 * jnp.arange(half_rot, dtype=F32) / ROT)
    angles = positions.astype(F32)[:, None] * frequency[None, :]
    cos_half, sin_half = jnp.cos(angles), jnp.sin(angles)
    cosine = jnp.concatenate([cos_half, cos_half, jnp.ones((rows, hd - ROT), F32)], axis=1)
    sine = jnp.concatenate([-sin_half, sin_half, jnp.zeros((rows, hd - ROT), F32)], axis=1)
    live = dict(out=out_held, near=out_near, mine=mine, given=given[1:], own=own, pair=pair)
    live["tables"] = (cosine, sine)
    live = lax.optimization_barrier(live)

    weights, arrived, ready, placed = [], {}, {}, {}
    handed, gathered = {}, {}
    chunks = len(sizes)
    places = [(c, i) for c, size in enumerate(sizes) for i in range(size)]
    last_stage = chunks + 2
    for stage in range(1, last_stage + 1):
        if stage <= chunks:
            held = [live["mine"][stage - 1]]
            for s in far[:-1]:
                held = held + [swap(w, "dp", s) for w in held]
            come = [swap(w, "dp", far[-1]) for w in held]
            with_out = [swap(w, "dp", 1) for w in live["out"][1:]] if stage == 1 else []
            come = hold(come + with_out, 150)
            weights.append(held + come[: len(held)])
            if stage == 1:
                live["out"] = live["out"] + [live.pop("near")] + come[len(held) :]
        if stage == 1:
            live["mine"] = live["mine"] + [lax.all_to_all(g, "hg", 0, 0, tiled=True) for g in live.pop("given")]
            pair = [over_t(over_h(live["pair"][0])), over_h(over_t(live["pair"][1]))]
            pair = after(pair, weights[0][-1])
            live["pair"] = pair + [swap(x, "hg", h_strides[-1]) for x in pair]
            own = live["own"]
            live["own"] = own + [swap(x, "hg", h_strides[-1]) for x in own]
        moved = [f for f, _, at, handover in finishing if at < handover == stage]
        come = [lax.all_to_all(live["placed"][f], "dp", 0, 0, tiled=True) for f in moved]
        sent = []
        for first, count, at, _ in finishing:
            c, i = places[first]
            if c + 2 == stage:
                partial = partner_call(live["pair"], live["weights"][c], rows, i, count)
                arrived[first] = swap(partial, "dp", 1)
                sent.append(first)
        if stage == chunks + 1:
            come = hold(come + [arrived[f] for f in sent], 60)
            arrived.update(zip(sent, come[len(moved) :]))
        handed.update(zip(moved, come))
        if stage == 2:
            held = split_call(meta, after(live["out"], partial), order_t)
            live["out"] = [swap(w, "tp", r) if r else w for w, r in zip(held, order_t)]
        for first, count, at, _ in finishing:
            if at == stage - 1 and first not in gathered:
                gathered[first] = [
                    head_gather(after(live["ready"][first], partial)[i], h_strides, t_strides, i % 2 == 0)
                    for i in range(count)
                ]
        for first, count, at, handover in finishing:
            if at == stage:
                c, i = places[first]
                come = live["arrived"].get(first)
                come = arrived[first] if come is None else come
                if 2 < at < last_stage:
                    come = after(come, partial)
                query, kv, placed[first] = finish_call(
                    meta, cached_lengths, owner_table, live["own"], live["weights"][c], come,
                    *live["tables"], cache_kv, i, first, cap, nd, (order_h, order_t),
                )
                ready[first] = attend_call(meta, cached_lengths, query, kv, cache_kv, first)
                if 2 < at < last_stage:
                    gathered[first] = [
                        head_gather(ready[first][n], h_strides, t_strides, n % 2 == 1) for n in range(count)
                    ]
                if at == handover:
                    blocks = after(placed[first], ready[first])
                    handed[first] = lax.all_to_all(blocks, "dp", 0, 0, tiled=True)
        if stage == last_stage:
            break
        live.update(weights=weights, arrived=arrived, ready=ready, placed=placed, handed=handed, gathered=gathered)
        live = lax.optimization_barrier(live)
        weights = list(live["weights"])
        arrived, ready, placed = dict(live["arrived"]), dict(live["ready"]), dict(live["placed"])
        handed, gathered = dict(live["handed"]), dict(live["gathered"])

    out_weights = live["out"]
    first, count, _, _ = finishing[-1]
    done = sorted(gathered)
    summed = None
    if done and cols % 128 == 0:
        parts = [p for f in done for head in gathered[f] for p in head]
        summed = output_call(meta, parts, out_weights, rows, 0, group, order_h, order_t)
    gathered[first] = [
        head_gather(ready[first][i], h_strides, t_strides, i % 2 == 0, summed) for i in range(count)
    ]
    collected = None
    if cols % 128 == 0:
        parts = [p for head in gathered[first] for p in head]
        pieces = output_call(meta, parts, out_weights, rows, first, group, order_h, order_t, summed, True)
        rels = [(h, t) for h in order_h for t in order_t]
        pieces = [plane_swap(p, h, t) if h or t else p for p, (h, t) in zip(pieces, rels)]
        if 2 * count == group:
            early = [handed[f] for f, _, _, _ in finishing[:-1]]
            collected = collect_call(early, group, 0)
            pieces[0] = after(pieces[0], collected)
        hidden_out = residual_call(meta, hidden_in[0, 0], pieces, offsets(all_d), order_h, order_t)
    else:
        parts = [p for f in sorted(gathered) for head in gathered[f] for p in head]
        summed = output_plain(place, hg, parts, out_weights, rows, group, order_h, order_t)
        summed = lax.all_to_all(
            summed.reshape(nh * nt, local_rows, nd * cols), ("hg", "tp"), 0, 0, tiled=True
        )
        summed = summed.reshape(nh, nt, local_rows, nd, cols).transpose(2, 3, 0, 1, 4).reshape(local_rows, width)
        hidden_out = (hidden_in[0, 0].astype(F32) + summed.astype(F32)).astype(BF16)
    if collected is not None:
        collected = collect_call([handed[first]], group, first, collected)
    else:
        collected = collect_call([handed[f] for f, _, _, _ in finishing], group, 0)
    return hidden_out[None, None], collected


def solution(mesh):
    return jax.shard_map(
        on_device,
        mesh=mesh,
        in_specs=(
            P("dp", "hg", "tp", None),
            P(),
            P(("dp", "hg"), None, "tp", None),
            P("tp", None, ("dp", "hg")),
            P("dp", "tp", None, None),
            P(),
            P(),
        ),
        out_specs=(P("dp", "hg", "tp", None), P("dp", ("tp", "hg"), None, None, None, None)),
        check_vma=False,
    )
```
